512 devices in a mesh: grp: 8 (over y, core), dev: 64 (over z, x).
Axes of the slice: x: 4, y: 4, z: 16, core: 2. Of those that a mesh axis runs over, the one named last changes fastest.
Arguments:
- right_side: float32 [512, 8192], P('grp', 'dev'), may hold values from -6 to 6
- previous: float32 [512, 8192], P('grp', 'dev'), may hold values from -4 to 4
- east_face: float32 [512, 8192], P('grp', 'dev'), may hold values from 0.5 to 10
- south_face: float32 [512, 8192], P('grp', 'dev'), may hold values from 0.5 to 10
- wet_mask: int32 [512, 8192], P('grp', 'dev'), may hold values from 0 to 1, as said below
Outputs:
- surface: float32 [512, 8192], P('grp', 'dev')
- residual: float32 [512, 8192], P('grp', 'dev')
The draws below stay inside these ranges and needn't reach their ends.
Inputs may be any that keep to these rules, and one draw needn't show every extreme that they name: `wet_mask`: dry cells form axis-aligned rectangles of 1 to 7 by 1 to 7 cells; each lies inside one aligned tile of 16 x 16 cells, one cell or more away from the tile's border, at most one rectangle a tile.
All inputs are finite; a program needn't handle non-finite values.
Results may differ from the reference program's by a relative error of at most 0.0003.
Values sent between devices are 32-bit elements; how exact they have to be, the bound alone decides.
No kernel may reach another device: no remote copies, remote signals or barrier semaphores. Data moves between devices by JAX's collectives and lax.ppermute only.
A program may use at most 64 MiB of HBM per device.

```python
import math
import jax
import jax.numpy as jnp

CYCLES = 2
PRE = 2
POST = 2
COARSE_SWEEPS = 4
NY = 512
NX = 8192


def draw_right_side(key, part):
    return jnp.clip(jax.random.normal(key, (NY, NX), jnp.float32), -6.0, 6.0)


def draw_wet_mask(key, part):
    subkeys = jax.random.split(key, 5)
    tiles_y = NY // 16
    tiles_x = NX // 16
    present = jax.random.randint(subkeys[0], (tiles_y, tiles_x), 0, 2)
    top_edge = jax.random.randint(subkeys[1], (tiles_y, tiles_x), 1, 8)
    row_span = jax.random.randint(subkeys[2], (tiles_y, tiles_x), 1, 8)
    left_edge = jax.random.randint(subkeys[3], (tiles_y, tiles_x), 1, 8)
    col_span = jax.random.randint(subkeys[4], (tiles_y, tiles_x), 1, 8)

    def spread(table):
        return jnp.repeat(jnp.repeat(table, 16, axis=0), 16, axis=1)
    local_row = (jnp.arange(NY, dtype=jnp.int32) % 16)[:, None]
    local_col = (jnp.arange(NX, dtype=jnp.int32) % 16)[None, :]
    top_full = spread(top_edge)
    left_full = spread(left_edge)
    inside_rows = (local_row >= top_full) & (local_row < top_full + spread(row_span))
    inside_cols = (local_col >= left_full) & (local_col < left_full + spread(col_span))
    dry_cell = spread(present) * (inside_rows & inside_cols).astype(jnp.int32)
    return (1 - dry_cell).astype(jnp.int32)


def block_scale(key, shape, cuts, least, largest):
    loudness = 1.0
    for axis_at, parts in cuts:
        draws = jax.random.uniform(jax.random.fold_in(jax.random.fold_in(key, 6), axis_at), (parts,), jnp.float32, least / len(cuts), largest / len(cuts))
        loudness = loudness * jnp.repeat(jnp.exp(draws), shape[axis_at] // parts).reshape((-1,) + (1,) * (len(shape) - 1 - axis_at))
    return loudness


def noise(own_key, shape, scale, bound, cuts=(), kind=jnp.bfloat16):
    result = scale * jax.random.normal(own_key, shape, jnp.float32)
    if cuts:
        result = result * block_scale(own_key, shape, cuts, -0.22, 0.18)
    return jnp.clip(result, -bound, bound).astype(kind)


def setup_inputs(seed: int = 0) -> dict:
    splits = jax.random.split(jax.random.key(seed), 6)
    return {
        "right_side": draw_right_side(jax.random.fold_in(splits[5], 71), 0),
        "previous": noise(splits[1], (NY, NX), 0.5, 4.0, ((0, 8), (1, 64)), jnp.float32),
        "east_face": jnp.clip(jnp.exp(math.log(10.0) - 2.9957323 * jax.random.uniform(splits[2], (NY, NX), jnp.float32) ** block_scale(splits[2], (NY, NX), ((0, 8), (1, 64)), -0.2, 0.2)), 0.5, 10.0),
        "south_face": jnp.clip(jnp.exp(math.log(10.0) - 2.9957323 * jax.random.uniform(splits[3], (NY, NX), jnp.float32) ** block_scale(splits[3], (NY, NX), ((0, 8), (1, 64)), -0.2, 0.2)), 0.5, 10.0),
        "wet_mask": draw_wet_mask(jax.random.fold_in(splits[5], 71), 0),
    }


relax_weight = 0.8
wet_mass = 2e-5


def coarsen_sum(values):
    row_count, col_count = values.shape
    return values.reshape(row_count // 2, 2, col_count // 2, 2).sum(axis=(1, 3))


def coarsen_links(coefficients):
    mass_term, east_link, west_link, south_link, north_link = coefficients
    return (coarsen_sum(mass_term),
            east_link[0::2, 1::2] + east_link[1::2, 1::2],
            west_link[0::2, 0::2] + west_link[1::2, 0::2],
            south_link[1::2, 0::2] + south_link[1::2, 1::2],
            north_link[0::2, 0::2] + north_link[0::2, 1::2])


def inverse_diagonal(coefficients):
    mass_term, east_link, west_link, south_link, north_link = coefficients
    return 1.0 / (mass_term + east_link + west_link + south_link + north_link)


def operate(padded, coefficients):
    mass_term, east_link, west_link, south_link, north_link = coefficients
    centre = padded[1:-1, 1:-1]
    return (mass_term * centre + east_link * (centre - padded[1:-1, 2:]) + west_link * (centre - padded[1:-1, :-2])
            + south_link * (centre - padded[2:, 1:-1]) + north_link * (centre - padded[:-2, 1:-1]))


def jacobi_sweep(values, padded, source, coefficients, inverse):
    return values + relax_weight * (source - operate(padded, coefficients)) * inverse


def zero_padded(values):
    return jnp.pad(values, 1)


def prolong(values):
    return jnp.repeat(jnp.repeat(values, 2, axis=0), 2, axis=1)


def smoothing(values, source, coefficients, inverse, sweeps, from_zero, padder):
    for sweep_index in range(sweeps):
        if from_zero and sweep_index == 0:
            values = relax_weight * source * inverse
        else:
            values = jacobi_sweep(values, padder(values), source, coefficients, inverse)
    return values


def descend(level_index, values, source, hierarchy, inverses, from_zero):
    if level_index == 4:
        values = smoothing(None, source, hierarchy[4], inverses[4], COARSE_SWEEPS, True, zero_padded)
        rest = source - operate(zero_padded(values), hierarchy[4])
        return values + relax_weight * jnp.sum(rest) / jnp.sum(hierarchy[4][0])
    coefficients = hierarchy[level_index]
    values = smoothing(values, source, coefficients, inverses[level_index], PRE, from_zero, zero_padded)
    remainder = coarsen_sum(source - operate(zero_padded(values), coefficients))
    values = values + prolong(descend(level_index + 1, None, remainder, hierarchy, inverses, True))
    return smoothing(values, source, coefficients, inverses[level_index], POST, False, zero_padded)


def reference(right_side, previous, east_face, south_face, wet_mask):
    wet = wet_mask.astype(jnp.float32)
    wet_pad = jnp.pad(wet, 1)
    east_pad = jnp.pad(east_face, 1)
    south_pad = jnp.pad(south_face, 1)
    east_link = east_face * wet * wet_pad[1:-1, 2:]
    west_link = east_pad[1:-1, :-2] * wet_pad[1:-1, :-2] * wet
    south_link = south_face * wet * wet_pad[2:, 1:-1]
    north_link = south_pad[:-2, 1:-1] * wet_pad[:-2, 1:-1] * wet
    mass_term = wet * wet_mass + (1.0 - wet)
    source = wet * right_side + (1.0 - wet) * previous
    hierarchy = [(mass_term, east_link, west_link, south_link, north_link)]
    for level_index in range(4):
        hierarchy.append(coarsen_links(hierarchy[-1]))
    inverses = [inverse_diagonal(coefficients) for coefficients in hierarchy]
    surface = previous
    for cycle_index in range(CYCLES):
        surface = descend(0, surface, source, hierarchy, inverses, False)
    residual = source - operate(zero_padded(surface), hierarchy[0])
    return surface, residual
```

```python
import jax
import jax.numpy as jnp
from jax import lax
from jax.experimental import pallas as pl
from jax.experimental.pallas import tpu as pltpu
from jax.sharding import Mesh
from jax.sharding import PartitionSpec as P

F32 = jnp.float32
RELAX = 0.8
WET_MASS = 2e-05
PAD = 8
CHUNK = 32
EAST, WEST, SOUTH, NORTH, MASS, RATE = range(6)


def lanes(shape):
    return lax.broadcasted_iota(jnp.int32, shape, len(shape) - 1)


def from_east(x, step):
    return pltpu.roll(x, x.shape[1] - step, 1)


def from_west(x, step):
    return pltpu.roll(x, step, 1)


def first_of_pair(x, step):
    return (lanes(x.shape) & step) == 0


def pair_sum(x, step):
    return x + jnp.where(first_of_pair(x, step), from_east(x, step), from_west(x, step))


def get(ref, start, count, *at):
    return jnp.concatenate([ref[(*at, h, pl.ds(start, count), slice(None))] for h in range(ref.shape[len(at)])], axis=1)


def get_strided(ref, start, count, *at):
    return jnp.concatenate(
        [ref[(*at, h, pl.ds(start, count, stride=2), slice(None))] for h in range(ref.shape[len(at)])], axis=1
    )


def put(ref, start, value, *at):
    for h in range(ref.shape[len(at)]):
        ref[(*at, h, pl.ds(start, value.shape[0]), slice(None))] = value[:, 128 * h : 128 * h + 128]


def chunks(low, high, size=CHUNK):
    return [(a, min(size, high - a)) for a in range(low, high, size)]


def clear(*refs):
    for ref in refs:
        ref[...] = jnp.zeros(ref.shape, F32)


def operate(v_ref, co, a, n, step):
    v = get(v_ref, PAD + a, n)
    out = (
        get(co, a, n, MASS) * v
        + get(co, a, n, EAST) * (v - from_east(v, step))
        + get(co, a, n, WEST) * (v - from_west(v, step))
        + get(co, a, n, SOUTH) * (v - get(v_ref, PAD + a + 1, n))
        + get(co, a, n, NORTH) * (v - get(v_ref, PAD + a - 1, n))
    )
    return v, out


def sweep(v_ref, to, co, b_ref, low, high, step):
    for a, n in chunks(low, high):
        v, out = operate(v_ref, co, a, n, step)
        rest = -out if b_ref is None else get(b_ref, a, n) - out
        put(to, PAD + a, v + rest * get(co, a, n, RATE))


def first_sweep(to, co, b_ref, low, high):
    for a, n in chunks(low, high):
        put(to, PAD + a, get(b_ref, a, n) * get(co, a, n, RATE))


def residual(v_ref, to, co, b_ref, low, high, step):
    for a, n in chunks(low, high):
        _, out = operate(v_ref, co, a, n, step)
        put(to, a, -out if b_ref is None else get(b_ref, a, n) - out)


def block_sum(fine, a, n, step, *at):
    return pair_sum(get_strided(fine, 2 * a, n, *at) + get_strided(fine, 2 * a + 1, n, *at), step)


def restrict(fine, to, low, high, step):
    for a, n in chunks(low // 2, high // 2):
        put(to, a, block_sum(fine, a, n, step))


def prolong(coarse, base, to, low, high):
    for a, n in chunks(low // 2, high // 2):
        value = get(coarse, PAD + a, n)
        for p in range(2):
            for h in range(to.shape[0]):
                part = value[:, 128 * h : 128 * h + 128]
                rows = pl.ds(PAD + 2 * a + p, n, stride=2)
                to[h, rows, :] = part if base is None else base[h, rows, :] + part


def diagonal(co, a, n):
    total = get(co, a, n, MASS)
    for k in (EAST, WEST, SOUTH, NORTH):
        total = total + get(co, a, n, k)
    return total


def coarsen(fine, to, rows, step):
    for a, n in chunks(0, rows):
        put(to, a, block_sum(fine, a, n, step, MASS), MASS)
        east = get_strided(fine, 2 * a, n, EAST) + get_strided(fine, 2 * a + 1, n, EAST)
        put(to, a, jnp.where(first_of_pair(east, step), from_east(east, step), east), EAST)
        west = get_strided(fine, 2 * a, n, WEST) + get_strided(fine, 2 * a + 1, n, WEST)
        put(to, a, jnp.where(first_of_pair(west, step), west, from_west(west, step)), WEST)
        put(to, a, pair_sum(get_strided(fine, 2 * a + 1, n, SOUTH), step), SOUTH)
        put(to, a, pair_sum(get_strided(fine, 2 * a, n, NORTH), step), NORTH)


def set_rate(co, rows):
    for a, n in chunks(0, rows):
        d = diagonal(co, a, n)
        put(co, a, RELAX / jnp.where(d > 0, d, 1.0), RATE)


def field(*shape):
    return jax.ShapeDtypeStruct(shape, F32)


def scratch(*shape):
    return pltpu.VMEM(shape, F32)


def call(body, outs, scratches, *args):
    vmem = pl.BlockSpec(memory_space=pltpu.VMEM)
    return pl.pallas_call(
        body,
        out_shape=outs,
        in_specs=[vmem] * len(args),
        out_specs=jax.tree.map(lambda _: vmem, outs),
        scratch_shapes=scratches,
        compiler_params=pltpu.CompilerParams(vmem_limit_bytes=28 * 1024 * 1024),
    )(*args)


def prepare(right, previous, east, south, mask, own, to_east, to_west):
    wet = mask[...] > 0
    own[0] = jnp.where(wet, east[...], 0.0)
    own[1] = jnp.where(wet, south[...], 0.0)
    own[2] = jnp.where(wet, right[...], previous[...])
    own[3] = previous[...]
    low = lanes((64, 128)) < 64
    for k in range(2):
        a, b = own[2 * k], pltpu.roll(own[2 * k + 1], 64, 1)
        to_east[k] = jnp.where(low, b, a)
        to_west[k] = jnp.where(low, a, b)


def widen(own, west, east, out):
    low = lanes((64, 128)) < 64
    for k in range(2):
        e, w = east[k], west[k]
        out[2 * k] = own[2 * k]
        out[2 * k + 1] = own[2 * k + 1]
        out[4 + 2 * k] = jnp.where(low, e, w)
        out[5 + 2 * k] = jnp.where(low, pltpu.roll(e, 64, 1), pltpu.roll(w, 64, 1))


def descend(v1_ref, v2_ref, b1_ref, b2_ref, b3_ref, co, rest, temp, ranges):
    (l0, h0), (l1, h1), (l2, h2), (l3, h3) = ranges
    restrict(rest[0], b1_ref, l0, h0, 1)
    first_sweep(temp[1], co[1], b1_ref, l1, h1)
    sweep(temp[1], v1_ref, co[1], b1_ref, l1, h1, 2)
    residual(v1_ref, rest[1], co[1], b1_ref, l1, h1, 2)
    restrict(rest[1], b2_ref, l1, h1, 2)
    first_sweep(temp[2], co[2], b2_ref, l2, h2)
    sweep(temp[2], v2_ref, co[2], b2_ref, l2, h2, 4)
    residual(v2_ref, rest[2], co[2], b2_ref, l2, h2, 4)
    restrict(rest[2], b3_ref, l3, h3, 4)


def first_leg(own, up, down, co0, co1, co2, b0, b1, b2, v0, v1, v2, packed, *temps):
    wet_ref, south_ref, t0, t1, t2, r0, r1, r2, b3, co3 = temps
    clear(wet_ref, south_ref, t0, t1, t2, v0, v1, v2)
    parts = (up, own, down)

    def window(k, a, n):
        ref, o = parts[a // 64], a % 64
        return jnp.concatenate([ref[k, o : o + n, :], ref[4 + k, o : o + n, :]], axis=1)

    for a, n in chunks(0, 192):
        put(wet_ref, PAD + a, jnp.where(window(0, a, n) > 0, 1.0, 0.0))
        put(v0, PAD + a, window(3, a, n))
        put(b0, a, window(2, a, n))
    for a, n in chunks(0, 192):
        wet = get(wet_ref, PAD + a, n)
        east = window(0, a, n) * from_east(wet, 1)
        south = window(1, a, n) * get(wet_ref, PAD + a + 1, n)
        put(co0, a, east, EAST)
        put(co0, a, from_west(east, 1), WEST)
        put(co0, a, south, SOUTH)
        put(south_ref, PAD + a, south)
        put(co0, a, wet * WET_MASS + (1.0 - wet), MASS)
    for a, n in chunks(0, 192):
        put(co0, a, get(south_ref, PAD + a - 1, n), NORTH)
    set_rate(co0, 192)
    coarsen(co0, co1, 96, 1)
    set_rate(co1, 96)
    coarsen(co1, co2, 48, 2)
    set_rate(co2, 48)
    coarsen(co2, co3, 24, 4)
    sweep(v0, t0, co0, b0, 0, 192, 1)
    sweep(t0, v0, co0, b0, 0, 192, 1)
    residual(v0, r0, co0, b0, 0, 192, 1)
    descend(
        v1, v2, b1, b2, b3, (co0, co1, co2), (r0, r1, r2), (t0, t1, t2), ((0, 192), (0, 96), (0, 48), (16, 32))
    )
    slot = lanes((8, 128)) & 7
    values = (
        b3[0, 8:16, :],
        co3[MASS, 0, 8:16, :],
        co3[EAST, 0, 8:16, :],
        co3[SOUTH, 0, 8:16, :],
        diagonal(co3, 8, 8)[:, :128],
    )
    out = jnp.zeros((8, 128), F32)
    for k, value in enumerate(values):
        out = jnp.where(slot == k, value, out)
    packed[...] = out


def fan_row(west, own, east, out):
    for g in range(out.shape[0]):
        out[g, 0] = west[...]
        out[g, 1] = own[...]
        out[g, 2] = east[...]


def spread(x, slot):
    y = jnp.where((lanes(x.shape) & 7) == slot, x, 0.0)
    for step in (1, 2, 4):
        y = pair_sum(y, step)
    return y


def inner_part(wide, to):
    to[0, pl.ds(PAD, 24), :] = wide[1, pl.ds(PAD + 8, 24), :]
    low = lanes((24, 128)) < 64
    to[1, pl.ds(PAD, 24), :] = jnp.where(low, wide[2, pl.ds(PAD + 8, 24), :], wide[0, pl.ds(PAD + 8, 24), :])


def solve_coarse(b3, b4, co3, co4, v3, s3, v4, s4, rest, shift):
    first_sweep(s3, co3, b3, 0, 40)
    sweep(s3, v3, co3, b3, 0, 40, 8)
    residual(v3, rest, co3, b3, 0, 40, 8)
    restrict(rest, b4, 0, 48, 8)
    first_sweep(s4, co4, b4, 0, 24)
    sweep(s4, v4, co4, b4, 0, 24, 16)
    sweep(v4, s4, co4, b4, 0, 24, 16)
    sweep(s4, v4, co4, b4, 0, 24, 16)
    if shift is not None:
        put(v4, PAD, get(v4, PAD, 24) + shift)
    prolong(v4, v3, v3, 0, 40)
    sweep(v3, s3, co3, b3, 0, 40, 8)
    sweep(s3, v3, co3, b3, 0, 40, 8)


def second_leg(gathered, co0, co1, co2, b0, b1, b2, v0, v1, v2, *others):
    (v0a, v0b, v1a, v1b, v2a, v2b, b1a, b1b, b2a, b2b, co3, co4, packed, *temps) = others
    (t0, s0, u0, t1, s1, u1, t2, s2, u2, r0, r1, r2, e3, u3, bn, b3, b4, v3, s3, w3, v4, s4, r3, south_ref) = temps
    clear(t0, s0, u0, t1, s1, u1, t2, s2, u2, e3, u3, v3, s3, w3, v4, s4, r3, south_ref, co4)
    clear(v0a, v0b, v1a, v1b, v2a, v2b)
    group = lax.axis_index("grp")
    for t in range(5):
        at = group + (t - 2)
        valid = jnp.logical_and(at >= 0, at < 8).astype(F32)
        at = jnp.clip(at, 0, 7)
        x = jnp.concatenate([gathered[at, k] for k in range(3)], axis=1) * valid
        row = 8 * t
        put(b3, row, spread(x, 0))
        put(co3, row, spread(x, 1), MASS)
        east = spread(x, 2)
        put(co3, row, east, EAST)
        put(co3, row, from_west(east, 8), WEST)
        south = spread(x, 3)
        put(co3, row, south, SOUTH)
        put(south_ref, PAD + row, south)
        d = spread(x, 4)
        put(co3, row, RELAX / jnp.where(d > 0, d, 1.0), RATE)
    for a, n in chunks(0, 40):
        put(co3, a, get(south_ref, PAD + a - 1, n), NORTH)
    coarsen(co3, co4, 20, 8)
    set_rate(co4, 24)

    put(v4, PAD, jnp.ones((24, 384), F32))
    for here, there in ((v4, s4), (s4, v4), (v4, s4), (s4, v4)):
        sweep(here, there, co4, None, 0, 24, 16)
    prolong(v4, None, w3, 0, 40)
    sweep(w3, s3, co3, None, 0, 40, 8)
    sweep(s3, w3, co3, None, 0, 40, 8)
    weight = w3[1, pl.ds(PAD + 16, 8), :]

    solve_coarse(b3, b4, co3, co4, v3, s3, v4, s4, r3, None)
    inner_part(v3, e3)
    put(v3, PAD, jnp.ones((40, 384), F32))
    sweep(v3, s3, co3, None, 0, 40, 8)
    sweep(s3, v3, co3, None, 0, 40, 8)
    inner_part(v3, u3)
    for base, coarse, b_ref, level in ((v2, e3, b2, 0), (None, u3, None, 1)):
        e2, e1, e0 = (t2, t1, t0) if level == 0 else (u2, u1, u0)
        prolong(coarse, base, e2, 0, 48)
        sweep(e2, s2, co2, b_ref, 0, 48, 4)
        sweep(s2, e2, co2, b_ref, 0, 48, 4)
        prolong(e2, None if base is None else v1, e1, 8, 88)
        sweep(e1, s1, co1, None if base is None else b1, 8, 88, 2)
        sweep(s1, e1, co1, None if base is None else b1, 8, 88, 2)
        prolong(e1, None if base is None else v0, e0, 32, 160)
        sweep(e0, s0, co0, None if base is None else b0, 32, 160, 1)
        sweep(s0, e0, co0, None if base is None else b0, 32, 160, 1)

    source = b3[1, 16:24, :]
    mass = co3[MASS, 1, 16:24, :]
    results = []
    for start, b_ref, x0, x1, x2, y1, y2 in ((t0, b0, v0a, v1a, v2a, b1a, b2a), (u0, None, v0b, v1b, v2b, b1b, b2b)):
        clear(s0, s1, s2)
        sweep(start, s0, co0, b_ref, 32, 160, 1)
        sweep(s0, x0, co0, b_ref, 32, 160, 1)
        residual(x0, r0, co0, b_ref, 32, 160, 1)
        descend(
            x1, x2, y1, y2, bn, (co0, co1, co2), (r0, r1, r2), (s0, s1, s2), ((32, 160), (16, 80), (8, 40), (16, 32))
        )
        results.append(bn[0, 8:16, :])
    place = lanes((8, 128))
    out = jnp.where((place & 7) == 0, results[0], jnp.where((place & 7) == 1, results[1], 0.0))
    sums = (mass, weight * source, weight * results[0], weight * results[1])
    for k, value in enumerate(sums):
        once = jnp.where((place & 7) == 0, value, 0.0)
        total = jnp.sum(jnp.sum(once, axis=0, keepdims=True), axis=1, keepdims=True)
        out = jnp.where(place == 8 * k + 6, total, out)
    for z in range(packed.shape[0]):
        packed[z] = out


def relay(gathered, out):
    z = lax.axis_index("z")
    last = gathered.shape[0] - 1
    own = gathered[z]
    before = gathered[jnp.maximum(z - 1, 0)]
    after = gathered[jnp.minimum(z + 1, last)]
    total = gathered[0]
    for k in range(1, last + 1):
        total = total + gathered[k]
    slot = lanes((8, 128)) & 7
    value = jnp.where(slot < 2, own, jnp.where(slot < 4, pltpu.roll(before, 2, 1), pltpu.roll(after, 4, 1)))
    value = jnp.where(slot < 6, value, total)
    for k in range(out.shape[0]):
        out[k] = value


def third_leg(gathered, co0, co1, co2, b0, v0a, v0b, v1a, v1b, v2a, v2b, b1a, b1b, b2a, b2b, co3, co4, *others):
    (surface, rest, *temps) = others
    (t0, s0, c0, t1, s1, c1, d1, t2, s2, c2, d2, e3, b3, b4, v3, s3, v4, s4, r3) = temps
    clear(t0, s0, c0, t1, s1, c1, t2, s2, c2, e3, v3, s3, v4, s4, r3)
    total = gathered[0]
    for k in range(1, gathered.shape[0]):
        total = total + gathered[k]
    place = lanes((1, 128))
    mass, sum1, sum2a, sum2b = (
        jnp.sum(jnp.where(place == 8 * k + 6, total[:1], 0.0), axis=1, keepdims=True) for k in range(4)
    )
    shift1 = RELAX * sum1 / mass
    shift2 = RELAX * (sum2a + shift1 * sum2b) / mass

    group, x = lax.axis_index("grp"), lax.axis_index("x")
    inner_west, inner_east = x > 0, x < 3
    at_west = jnp.where(inner_west, x - 1, 3)
    at_east = jnp.where(inner_east, x + 1, 0)
    for t in range(5):
        g = 4 * jnp.clip(group + (t - 2), 0, 7)
        w, o, e = gathered[g + at_west], gathered[g + x], gathered[g + at_east]
        w = jnp.where(inner_west, w, pltpu.roll(w, 126, 1))
        e = jnp.where(inner_east, e, pltpu.roll(e, 124, 1))
        both = jnp.concatenate([w, o, e], axis=1)
        put(b3, 8 * t, spread(both + shift1 * from_east(both, 1), 0))
    solve_coarse(b3, b4, co3, co4, v3, s3, v4, s4, r3, shift2)
    inner_part(v3, e3)

    def combine(to, first, second, offset, low, high):
        for a, n in chunks(offset + low, offset + high):
            put(to, a, get(first, a, n) + shift1 * get(second, a, n))

    combine(c2, v2a, v2b, PAD, 8, 40)
    combine(d2, b2a, b2b, 0, 8, 40)
    combine(c1, v1a, v1b, PAD, 24, 72)
    combine(d1, b1a, b1b, 0, 24, 72)
    combine(c0, v0a, v0b, PAD, 56, 136)
    prolong(e3, c2, t2, 8, 40)
    sweep(t2, s2, co2, d2, 8, 40, 4)
    sweep(s2, t2, co2, d2, 8, 40, 4)
    prolong(t2, c1, t1, 24, 72)
    sweep(t1, s1, co1, d1, 24, 72, 2)
    sweep(s1, t1, co1, d1, 24, 72, 2)
    prolong(t1, c0, t0, 56, 136)
    sweep(t0, s0, co0, b0, 56, 136, 1)
    sweep(s0, t0, co0, b0, 56, 136, 1)
    surface[...] = t0[0, pl.ds(PAD + 64, 64), :]
    for a, n in chunks(64, 128):
        _, out = operate(t0, co0, a, n, 1)
        rest[a - 64 : a - 64 + n, :] = b0[0, a : a + n, :] - out[:, :128]


def shards(right_side, previous, east_face, south_face, wet_mask):
    dev = ("z", "x")
    to_next = [(i, i + 1) for i in range(63)]
    to_last = [(j, i) for i, j in to_next]
    own, to_east, to_west = call(
        prepare,
        (field(4, 64, 128), field(2, 64, 128), field(2, 64, 128)),
        [],
        right_side,
        previous,
        east_face,
        south_face,
        wet_mask,
    )
    west = lax.ppermute(to_east, dev, to_next)
    east = lax.ppermute(to_west, dev, to_last)
    own = call(widen, field(8, 64, 128), [], own, west, east)
    up = lax.ppermute(own, "grp", to_next[:7])
    down = lax.ppermute(own, "grp", to_last[:7])

    def rows(count, planes=2):
        return field(planes, count, 128)

    def shifted(count, planes=2):
        return field(planes, count + 2 * PAD, 128)

    def as_scratch(*fields):
        return [scratch(*f.shape) for f in fields]

    co = [field(6, 2, count, 128) for count in (192, 96, 48)]
    *kept, packed = call(
        first_leg,
        (*co, rows(192), rows(96), rows(48), shifted(192), shifted(96), shifted(48), field(8, 128)),
        as_scratch(
            shifted(192),
            shifted(192),
            shifted(192),
            shifted(96),
            shifted(48),
            rows(192),
            rows(96),
            rows(48),
            rows(24),
            field(6, 2, 24, 128),
        ),
        own,
        up,
        down,
    )
    west = lax.ppermute(packed, dev, to_next)
    east = lax.ppermute(packed, dev, to_last)
    gathered = call(fan_row, field(8, 3, 8, 128), [], west, packed, east)
    gathered = lax.all_to_all(gathered, "grp", 0, 0, tiled=True)
    wide = [shifted(40, 3), shifted(40, 3), shifted(40, 3), shifted(24, 3), shifted(24, 3)]
    *second, packed = call(
        second_leg,
        (
            shifted(192),
            shifted(192),
            shifted(96),
            shifted(96),
            shifted(48),
            shifted(48),
            rows(96),
            rows(96),
            rows(48),
            rows(48),
            field(6, 3, 40, 128),
            field(6, 3, 24, 128),
            field(16, 8, 128),
        ),
        as_scratch(
            *[shifted(192)] * 3,
            *[shifted(96)] * 3,
            *[shifted(48)] * 3,
            rows(192),
            rows(96),
            rows(48),
            shifted(24),
            shifted(24),
            rows(24),
            rows(40, 3),
            rows(24, 3),
            *wide,
            rows(48, 3),
            shifted(40, 3),
        ),
        gathered,
        *kept,
    )
    gathered = lax.all_to_all(packed, "z", 0, 0, tiled=True)
    gathered = call(relay, field(32, 8, 128), [], gathered)
    gathered = lax.all_to_all(gathered, ("grp", "x"), 0, 0, tiled=True)
    surface, rest = call(
        third_leg,
        (field(64, 128), field(64, 128)),
        as_scratch(
            *[shifted(192)] * 3,
            *[shifted(96)] * 3,
            rows(96),
            *[shifted(48)] * 3,
            rows(48),
            shifted(24),
            rows(40, 3),
            rows(24, 3),
            shifted(40, 3),
            shifted(40, 3),
            shifted(24, 3),
            shifted(24, 3),
            rows(48, 3),
        ),
        gathered,
        *kept[:4],
        *second,
    )
    return surface, rest


def solution(mesh):
    split = Mesh(mesh.devices.reshape(8, 16, 4), ("grp", "z", "x"))
    placed = P("grp", ("z", "x"))
    return jax.shard_map(shards, mesh=split, in_specs=(placed,) * 5, out_specs=(placed,) * 2, check_vma=False)
```

```python
import jax
import jax.numpy as jnp
from jax import lax
from jax.experimental import pallas as pl
from jax.experimental.pallas import tpu as pltpu
from jax.sharding import Mesh
from jax.sharding import PartitionSpec as P

F32 = jnp.float32
RELAX = 0.8
WET_MASS = 2e-05
PAD = 8
CHUNK = 32
EAST, WEST, SOUTH, NORTH, MASS, RATE = range(6)


def lanes(shape):
    return lax.broadcasted_iota(jnp.int32, shape, len(shape) - 1)


def from_east(x, step):
    return pltpu.roll(x, x.shape[1] - step, 1)


def from_west(x, step):
    return pltpu.roll(x, step, 1)


def first_of_pair(x, step):
    return (lanes(x.shape) & step) == 0


def pair_sum(x, step):
    return x + jnp.where(first_of_pair(x, step), from_east(x, step), from_west(x, step))


def get(ref, start, count, *at):
    return jnp.concatenate([ref[(*at, h, pl.ds(start, count), slice(None))] for h in range(ref.shape[len(at)])], axis=1)


def get_strided(ref, start, count, *at):
    return jnp.concatenate(
        [ref[(*at, h, pl.ds(start, count, stride=2), slice(None))] for h in range(ref.shape[len(at)])], axis=1
    )


def put(ref, start, value, *at):
    for h in range(ref.shape[len(at)]):
        ref[(*at, h, pl.ds(start, value.shape[0]), slice(None))] = value[:, 128 * h : 128 * h + 128]


def chunks(low, high, size=CHUNK):
    return [(a, min(size, high - a)) for a in range(low, high, size)]


def operate(v_ref, co, a, n, step):
    v = get(v_ref, PAD + a, n)
    out = (
        get(co, a, n, MASS) * v
        + get(co, a, n, EAST) * (v - from_east(v, step))
        + get(co, a, n, WEST) * (v - from_west(v, step))
        + get(co, a, n, SOUTH) * (v - get(v_ref, PAD + a + 1, n))
        + get(co, a, n, NORTH) * (v - get(v_ref, PAD + a - 1, n))
    )
    return v, out


def sweep(v_ref, to, co, b_ref, low, high, step):
    for a, n in chunks(low, high):
        v, out = operate(v_ref, co, a, n, step)
        rest = -out if b_ref is None else get(b_ref, a, n) - out
        put(to, PAD + a, v + rest * get(co, a, n, RATE))


def first_sweep(to, co, b_ref, low, high):
    for a, n in chunks(low, high):
        put(to, PAD + a, get(b_ref, a, n) * get(co, a, n, RATE))


def residual(v_ref, to, co, b_ref, low, high, step):
    for a, n in chunks(low, high):
        _, out = operate(v_ref, co, a, n, step)
        put(to, a, -out if b_ref is None else get(b_ref, a, n) - out)


def block_sum(fine, a, n, step, *at):
    return pair_sum(get_strided(fine, 2 * a, n, *at) + get_strided(fine, 2 * a + 1, n, *at), step)


def restrict(fine, to, low, high, step):
    for a, n in chunks(low // 2, high // 2):
        put(to, a, block_sum(fine, a, n, step))


def prolong(coarse, base, to, low, high):
    for a, n in chunks(low // 2, high // 2):
        value = get(coarse, PAD + a, n)
        for p in range(2):
            for h in range(to.shape[0]):
                part = value[:, 128 * h : 128 * h + 128]
                rows = pl.ds(PAD + 2 * a + p, n, stride=2)
                to[h, rows, :] = part if base is None else base[h, rows, :] + part


def diagonal(co, a, n):
    total = get(co, a, n, MASS)
    for k in (EAST, WEST, SOUTH, NORTH):
        total = total + get(co, a, n, k)
    return total


def coarsen(fine, to, rows, step):
    for a, n in chunks(0, rows):
        put(to, a, block_sum(fine, a, n, step, MASS), MASS)
        east = get_strided(fine, 2 * a, n, EAST) + get_strided(fine, 2 * a + 1, n, EAST)
        put(to, a, jnp.where(first_of_pair(east, step), from_east(east, step), east), EAST)
        west = get_strided(fine, 2 * a, n, WEST) + get_strided(fine, 2 * a + 1, n, WEST)
        put(to, a, jnp.where(first_of_pair(west, step), west, from_west(west, step)), WEST)
        put(to, a, pair_sum(get_strided(fine, 2 * a + 1, n, SOUTH), step), SOUTH)
        put(to, a, pair_sum(get_strided(fine, 2 * a, n, NORTH), step), NORTH)


def set_rate(co, rows):
    for a, n in chunks(0, rows):
        d = diagonal(co, a, n)
        put(co, a, RELAX / jnp.where(d > 0, d, 1.0), RATE)


STATE = (208, 112, 64, 96, 48, 192)
STATE_ROWS = sum(STATE)


def state_of(ref):
    starts = [sum(STATE[:k]) for k in range(6)]
    return [ref.at[:, pl.ds(start, count), :] for start, count in zip(starts, STATE)]


def field(*shape):
    return jax.ShapeDtypeStruct(shape, F32)


def scratch(*shape):
    return pltpu.VMEM(shape, F32)


def call(body, outs, scratches, *args, at=pltpu.VMEM, cycles=1000, room=12):
    vmem = pl.BlockSpec(memory_space=pltpu.VMEM)
    return pl.pallas_call(
        body,
        out_shape=outs,
        in_specs=[pl.BlockSpec(memory_space=at)] * len(args),
        out_specs=jax.tree.map(lambda _: vmem, outs),
        scratch_shapes=scratches,
        cost_estimate=pl.CostEstimate(flops=2000 * cycles, bytes_accessed=2000 * cycles, transcendentals=0),
        compiler_params=pltpu.CompilerParams(vmem_limit_bytes=room * 1024 * 1024),
    )(*args)


def prepare(*refs):
    sources, (own, to_east, to_west), temps, arrived = refs[:5], refs[5:8], refs[8:13], refs[13]
    copies = [pltpu.make_async_copy(sources[k], temps[k], arrived.at[k]) for k in range(5)]
    for copy in copies:
        copy.start()
    for copy in copies:
        copy.wait()
    right, previous, east, south, mask = temps
    wet = mask[...] > 0
    own[0] = jnp.where(wet, east[...], 0.0)
    own[1] = jnp.where(wet, south[...], 0.0)
    own[2] = jnp.where(wet, right[...], previous[...])
    own[3] = previous[...]
    low = lanes((64, 128)) < 64
    for k in range(2):
        a, b = own[2 * k], pltpu.roll(own[2 * k + 1], 64, 1)
        to_east[k] = jnp.where(low, b, a)
        to_west[k] = jnp.where(low, a, b)


def widen(own, west, east, out):
    low = lanes((64, 128)) < 64
    for k in range(2):
        e, w = east[k], west[k]
        out[2 * k] = own[2 * k]
        out[2 * k + 1] = own[2 * k + 1]
        out[4 + 2 * k] = jnp.where(low, e, w)
        out[5 + 2 * k] = jnp.where(low, pltpu.roll(e, 64, 1), pltpu.roll(w, 64, 1))


def descend(v1_ref, v2_ref, b1_ref, b2_ref, b3_ref, co, rest, temp, ranges):
    (l0, h0), (l1, h1), (l2, h2), (l3, h3) = ranges
    restrict(rest[0], b1_ref, l0, h0, 1)
    first_sweep(temp[1], co[1], b1_ref, l1, h1)
    sweep(temp[1], v1_ref, co[1], b1_ref, l1, h1, 2)
    residual(v1_ref, rest[1], co[1], b1_ref, l1, h1, 2)
    restrict(rest[1], b2_ref, l1, h1, 2)
    first_sweep(temp[2], co[2], b2_ref, l2, h2)
    sweep(temp[2], v2_ref, co[2], b2_ref, l2, h2, 4)
    residual(v2_ref, rest[2], co[2], b2_ref, l2, h2, 4)
    restrict(rest[2], b3_ref, l3, h3, 4)


def first_leg(own, up, down, co0, co1, co2, state, co3, packed, *temps):
    v0, v1, v2, b1, b2, b0 = state_of(state)
    wet_ref, south_ref, t0, t1, t2, r0, r1, r2, b3 = temps
    parts = (up, own, down)

    def window(k, a, n):
        ref, o = parts[a // 64], a % 64
        return jnp.concatenate([ref[k, o : o + n, :], ref[4 + k, o : o + n, :]], axis=1)

    for a, n in chunks(0, 192):
        put(wet_ref, PAD + a, jnp.where(window(0, a, n) > 0, 1.0, 0.0))
        put(v0, PAD + a, window(3, a, n))
        put(b0, a, window(2, a, n))
    for a, n in chunks(0, 192):
        wet = get(wet_ref, PAD + a, n)
        east = window(0, a, n) * from_east(wet, 1)
        south = window(1, a, n) * get(wet_ref, PAD + a + 1, n)
        put(co0, a, east, EAST)
        put(co0, a, from_west(east, 1), WEST)
        put(co0, a, south, SOUTH)
        put(south_ref, PAD + a, south)
        put(co0, a, wet * WET_MASS + (1.0 - wet), MASS)
    for a, n in chunks(0, 192):
        put(co0, a, get(south_ref, PAD + a - 1, n), NORTH)
    set_rate(co0, 192)
    coarsen(co0, co1, 96, 1)
    set_rate(co1, 96)
    coarsen(co1, co2, 48, 2)
    set_rate(co2, 48)
    coarsen(co2, co3, 24, 4)
    set_rate(co3, 24)
    sweep(v0, t0, co0, b0, 0, 192, 1)
    sweep(t0, v0, co0, b0, 0, 192, 1)
    residual(v0, r0, co0, b0, 0, 192, 1)
    descend(
        v1, v2, b1, b2, b3, (co0, co1, co2), (r0, r1, r2), (t0, t1, t2), ((0, 192), (0, 96), (0, 48), (16, 32))
    )
    slot = lanes((8, 128)) & 7
    values = (
        b3[0, 8:16, :],
        co3[MASS, 0, 8:16, :],
        co3[EAST, 0, 8:16, :],
        co3[SOUTH, 0, 8:16, :],
        diagonal(co3, 8, 8)[:, :128],
    )
    out = jnp.zeros((8, 128), F32)
    for k, value in enumerate(values):
        out = jnp.where(slot == k, value, out)
    packed[...] = out


def fan(own, crossed, out):
    for k in range(out.shape[0]):
        out[k, 0] = own[...]
        out[k, 1] = crossed[...]


def ascend(coarse, bases, sources, to, temp, co):
    ranges = ((32, 160), (8, 88), (0, 48))
    for level in (2, 1, 0):
        low, high = ranges[level]
        step = 1 << level
        prolong(coarse, bases[level], to[level], low, high)
        sweep(to[level], temp[level], co[level], sources[level], low, high, step)
        sweep(temp[level], to[level], co[level], sources[level], low, high, step)
        coarse = to[level]


def second_descent(start, source, kept, rest, temp, co):
    v0, v1, v2, b1, b2, b3 = kept
    sweep(start, temp[0], co[0], source, 32, 160, 1)
    sweep(temp[0], v0, co[0], source, 32, 160, 1)
    residual(v0, rest[0], co[0], source, 32, 160, 1)
    descend(v1, v2, b1, b2, b3, co, rest, temp, ((32, 160), (16, 80), (8, 40), (16, 32)))


def response(co0, co1, co2, co3, state, packed, *temps):
    v0, v1, v2, b1, b2, _ = state_of(state)
    t0, s0, t1, s1, t2, s2, v3, s3, r0, r1, r2, b3 = temps
    put(v3, PAD, jnp.ones((24, 256), F32))
    sweep(v3, s3, co3, None, 0, 24, 8)
    sweep(s3, v3, co3, None, 0, 24, 8)
    none, co = (None, None, None), (co0, co1, co2)
    ascend(v3, none, none, (t0, t1, t2), (s0, s1, s2), co)
    second_descent(t0, None, (v0, v1, v2, b1, b2, b3), (r0, r1, r2), (s0, s1, s2), co)
    packed[...] = b3[0, 8:16, :]


def neighbours():
    group, x = lax.axis_index("grp"), lax.axis_index("x")
    inner_west, inner_east = x > 0, x < 3
    return group, x, inner_west, inner_east, jnp.where(inner_west, x - 1, 3), jnp.where(inner_east, x + 1, 0)


def spread(x, slot):
    y = jnp.where((lanes(x.shape) & 7) == slot, x, 0.0)
    for step in (1, 2, 4):
        y = pair_sum(y, step)
    return y


def inner_part(wide, to):
    to[0, pl.ds(PAD, 24), :] = wide[1, pl.ds(PAD + 8, 24), :]
    low = lanes((24, 128)) < 64
    to[1, pl.ds(PAD, 24), :] = jnp.where(low, wide[2, pl.ds(PAD + 8, 24), :], wide[0, pl.ds(PAD + 8, 24), :])


def solve_coarse(b3, b4, co3, co4, v3, s3, v4, s4, rest, shift):
    first_sweep(s3, co3, b3, 0, 40)
    sweep(s3, v3, co3, b3, 0, 40, 8)
    residual(v3, rest, co3, b3, 0, 40, 8)
    restrict(rest, b4, 0, 48, 8)
    first_sweep(s4, co4, b4, 0, 24)
    sweep(s4, v4, co4, b4, 0, 24, 16)
    sweep(v4, s4, co4, b4, 0, 24, 16)
    sweep(s4, v4, co4, b4, 0, 24, 16)
    if shift is not None:
        put(v4, PAD, get(v4, PAD, 24) + shift)
    prolong(v4, v3, v3, 0, 40)
    sweep(v3, s3, co3, b3, 0, 40, 8)
    sweep(s3, v3, co3, b3, 0, 40, 8)


def second_leg(gathered, responded, co0, co1, co2, before, co3, co4, after, packed, *temps):
    v0, v1, v2, b1, b2, b0 = state_of(before)
    v0a, v1a, v2a, b1a, b2a, _ = state_of(after)
    (t0, s0, t1, s1, t2, s2, r0, r1, r2, e3, bn, b3, b4, v3, s3, w3, v4, s4, r3, south_ref) = temps
    group, own, inner_west, inner_east, at_west, at_east = neighbours()
    at_west = 2 * at_west + jnp.where(inner_west, 0, 1)
    at_east = 2 * at_east + jnp.where(inner_east, 0, 1)
    for t in range(5):
        at = group + (t - 2)
        valid = jnp.logical_and(at >= 0, at < 8).astype(F32)
        at = 8 * jnp.clip(at, 0, 7)
        x = jnp.concatenate([gathered[at + k] for k in (at_west, 2 * own, at_east)], axis=1) * valid
        row = 8 * t
        put(b3, row, spread(x, 0))
        put(co3, row, spread(x, 1), MASS)
        east = spread(x, 2)
        put(co3, row, east, EAST)
        put(co3, row, from_west(east, 8), WEST)
        south = spread(x, 3)
        put(co3, row, south, SOUTH)
        put(south_ref, PAD + row, south)
        d = spread(x, 4)
        put(co3, row, RELAX / jnp.where(d > 0, d, 1.0), RATE)
    for a, n in chunks(0, 40):
        put(co3, a, get(south_ref, PAD + a - 1, n), NORTH)
    coarsen(co3, co4, 20, 8)
    set_rate(co4, 24)

    put(v4, PAD, jnp.ones((24, 384), F32))
    for here, there in ((v4, s4), (s4, v4), (v4, s4), (s4, v4)):
        sweep(here, there, co4, None, 0, 24, 16)
    prolong(v4, None, w3, 0, 40)
    sweep(w3, s3, co3, None, 0, 40, 8)
    sweep(s3, w3, co3, None, 0, 40, 8)
    weight = w3[1, pl.ds(PAD + 16, 8), :]

    solve_coarse(b3, b4, co3, co4, v3, s3, v4, s4, r3, None)
    inner_part(v3, e3)
    co = (co0, co1, co2)
    ascend(e3, (v0, v1, v2), (b0, b1, b2), (t0, t1, t2), (s0, s1, s2), co)
    second_descent(t0, b0, (v0a, v1a, v2a, b1a, b2a, bn), (r0, r1, r2), (s0, s1, s2), co)
    result = bn[0, 8:16, :]
    place = lanes((8, 128))
    slot = place & 7
    out = jnp.where(slot == 0, result, jnp.where(slot == 1, responded[...], 0.0))
    mass = co3[MASS, 1, 16:24, :]
    sums = (mass, weight * b3[1, 16:24, :], weight * result, weight * responded[...])
    for k, value in enumerate(sums):
        once = jnp.where(slot == 0, value, 0.0)
        total = jnp.sum(jnp.sum(once, axis=0, keepdims=True), axis=1, keepdims=True)
        out = jnp.where(place == 8 * k + 6, total, out)
    for z in range(packed.shape[0]):
        packed[z] = out


def relay(gathered, out):
    z = lax.axis_index("z")
    last = gathered.shape[0] - 1
    own = gathered[z]
    before = gathered[jnp.maximum(z - 1, 0)]
    after = gathered[jnp.minimum(z + 1, last)]
    total = gathered[0]
    for k in range(1, last + 1):
        total = total + gathered[k]
    slot = lanes((8, 128)) & 7
    value = jnp.where(slot < 2, own, jnp.where(slot < 4, pltpu.roll(before, 2, 1), pltpu.roll(after, 4, 1)))
    value = jnp.where(slot < 6, value, total)
    for k in range(out.shape[0]):
        out[k] = value


def third_leg(gathered, co0, co1, co2, before, co3, co4, after, beside, *others):
    b0 = state_of(before)[5]
    v0a, v1a, v2a, b1a, b2a, _ = state_of(after)
    v0b, v1b, v2b, b1b, b2b, _ = state_of(beside)
    (surface, rest, *temps) = others
    (t0, s0, c0, t1, s1, c1, d1, t2, s2, c2, d2, e3, b3, b4, v3, s3, v4, s4, r3) = temps
    total = gathered[0]
    for k in range(1, gathered.shape[0]):
        total = total + gathered[k]
    place = lanes((1, 128))
    mass, sum1, sum2a, sum2b = (
        jnp.sum(jnp.where(place == 8 * k + 6, total[:1], 0.0), axis=1, keepdims=True) for k in range(4)
    )
    shift1 = RELAX * sum1 / mass
    shift2 = RELAX * (sum2a + shift1 * sum2b) / mass

    group, x, inner_west, inner_east, at_west, at_east = neighbours()
    for t in range(5):
        g = 4 * jnp.clip(group + (t - 2), 0, 7)
        w, o, e = gathered[g + at_west], gathered[g + x], gathered[g + at_east]
        w = jnp.where(inner_west, w, pltpu.roll(w, 126, 1))
        e = jnp.where(inner_east, e, pltpu.roll(e, 124, 1))
        both = jnp.concatenate([w, o, e], axis=1)
        put(b3, 8 * t, spread(both + shift1 * from_east(both, 1), 0))
    solve_coarse(b3, b4, co3, co4, v3, s3, v4, s4, r3, shift2)
    inner_part(v3, e3)

    def combine(to, first, second, offset, low, high):
        for a, n in chunks(offset + low, offset + high):
            put(to, a, get(first, a, n) + shift1 * get(second, a, n))

    combine(c2, v2a, v2b, PAD, 8, 40)
    combine(d2, b2a, b2b, 0, 8, 40)
    combine(c1, v1a, v1b, PAD, 24, 72)
    combine(d1, b1a, b1b, 0, 24, 72)
    combine(c0, v0a, v0b, PAD, 56, 136)
    prolong(e3, c2, t2, 8, 40)
    sweep(t2, s2, co2, d2, 8, 40, 4)
    sweep(s2, t2, co2, d2, 8, 40, 4)
    prolong(t2, c1, t1, 24, 72)
    sweep(t1, s1, co1, d1, 24, 72, 2)
    sweep(s1, t1, co1, d1, 24, 72, 2)
    prolong(t1, c0, t0, 56, 136)
    sweep(t0, s0, co0, b0, 56, 136, 1)
    sweep(s0, t0, co0, b0, 56, 136, 1)
    surface[...] = t0[0, pl.ds(PAD + 64, 64), :]
    for a, n in chunks(64, 128):
        _, out = operate(t0, co0, a, n, 1)
        rest[a - 64 : a - 64 + n, :] = b0[0, a : a + n, :] - out[:, :128]


def shards(right_side, previous, east_face, south_face, wet_mask):
    dev = ("z", "x")
    to_next = [(i, i + 1) for i in range(63)]
    to_last = [(j, i) for i, j in to_next]
    own, to_east, to_west = call(
        prepare,
        (field(4, 64, 128), field(2, 64, 128), field(2, 64, 128)),
        [*[scratch(64, 128)] * 4, pltpu.VMEM((64, 128), jnp.int32), pltpu.SemaphoreType.DMA((5,))],
        right_side,
        previous,
        east_face,
        south_face,
        wet_mask,
        at=pltpu.HBM,
        room=60,
    )
    west = lax.ppermute(to_east, dev, to_next)
    east = lax.ppermute(to_west, dev, to_last)
    own = call(widen, field(8, 64, 128), [], own, west, east)
    up = lax.ppermute(own, "grp", to_next[:7])
    down = lax.ppermute(own, "grp", to_last[:7])

    def rows(count, planes=2):
        return field(planes, count, 128)

    def shifted(count, planes=2):
        return field(planes, count + 2 * PAD, 128)

    def as_scratch(*fields):
        return [scratch(*f.shape) for f in fields]

    co = [field(6, 2, count, 128) for count in (192, 96, 48, 24)]
    fine = [shifted(count) for count in (192, 96, 48)]
    sources = [rows(count) for count in (192, 96, 48)]
    state = rows(STATE_ROWS)
    *kept, near, packed = call(
        first_leg,
        (*co[:3], state, co[3], field(8, 128)),
        as_scratch(fine[0], fine[0], *fine, *sources, rows(24)),
        own,
        up,
        down,
    )
    crossings = [(4 * z + 3, 4 * z + 7) for z in range(15)] + [(4 * z + 4, 4 * z) for z in range(15)]
    crossed = lax.ppermute(packed, dev, crossings)
    beside, responded = call(
        response,
        (state, field(8, 128)),
        as_scratch(*[f for f in fine for _ in range(2)], shifted(24), shifted(24), *sources, rows(24)),
        *kept[:3],
        near,
        cycles=3000,
    )
    gathered = call(fan, field(32, 2, 8, 128), [], packed, crossed)
    gathered = lax.all_to_all(gathered, ("grp", "x"), 0, 0, tiled=True).reshape(64, 8, 128)
    coarse = [shifted(40, 3), shifted(40, 3), shifted(40, 3), shifted(24, 3), shifted(24, 3)]
    *second, packed = call(
        second_leg,
        (field(6, 3, 40, 128), field(6, 3, 24, 128), state, field(16, 8, 128)),
        as_scratch(
            *[f for f in fine for _ in range(2)],
            *sources,
            shifted(24),
            rows(24),
            rows(40, 3),
            rows(24, 3),
            *coarse,
            rows(48, 3),
            shifted(40, 3),
        ),
        gathered,
        responded,
        *kept,
    )
    gathered = lax.all_to_all(packed, "z", 0, 0, tiled=True)
    gathered = call(relay, field(32, 8, 128), [], gathered)
    gathered = lax.all_to_all(gathered, ("grp", "x"), 0, 0, tiled=True)
    surface, rest = call(
        third_leg,
        (field(64, 128), field(64, 128)),
        as_scratch(
            *[shifted(192)] * 3,
            *[shifted(96)] * 3,
            rows(96),
            *[shifted(48)] * 3,
            rows(48),
            shifted(24),
            rows(40, 3),
            rows(24, 3),
            shifted(40, 3),
            shifted(40, 3),
            shifted(24, 3),
            shifted(24, 3),
            rows(48, 3),
        ),
        gathered,
        *kept,
        *second,
        beside,
    )
    return surface, rest


def solution(mesh):
    split = Mesh(mesh.devices.reshape(8, 16, 4), ("grp", "z", "x"))
    placed = P("grp", ("z", "x"))
    return jax.shard_map(shards, mesh=split, in_specs=(placed,) * 5, out_specs=(placed,) * 2, check_vma=False)
```

```python
import jax
import jax.numpy as jnp
from jax import lax
from jax.experimental import pallas as pl
from jax.experimental.pallas import tpu as pltpu
from jax.sharding import Mesh
from jax.sharding import PartitionSpec as P

F32 = jnp.float32
RELAX = 0.8
WET_MASS = 2e-05
PAD = 8
CHUNK = 32
EAST, WEST, SOUTH, NORTH, MASS, RATE = range(6)


def lanes(shape):
    return lax.broadcasted_iota(jnp.int32, shape, len(shape) - 1)


def from_east(x, step):
    return pltpu.roll(x, x.shape[1] - step, 1)


def from_west(x, step):
    return pltpu.roll(x, step, 1)


def first_of_pair(x, step):
    return (lanes(x.shape) & step) == 0


def pair_sum(x, step):
    return x + jnp.where(first_of_pair(x, step), from_east(x, step), from_west(x, step))


def get(ref, start, count, *at):
    return jnp.concatenate([ref[(*at, h, pl.ds(start, count), slice(None))] for h in range(ref.shape[len(at)])], axis=1)


def get_strided(ref, start, count, *at):
    return jnp.concatenate(
        [ref[(*at, h, pl.ds(start, count, stride=2), slice(None))] for h in range(ref.shape[len(at)])], axis=1
    )


def put(ref, start, value, *at):
    for h in range(ref.shape[len(at)]):
        ref[(*at, h, pl.ds(start, value.shape[0]), slice(None))] = value[:, 128 * h : 128 * h + 128]


def chunks(low, high, size=CHUNK):
    return [(a, min(size, high - a)) for a in range(low, high, size)]


def operate(v_ref, co, a, n, step):
    v = get(v_ref, PAD + a, n)
    out = (
        get(co, a, n, MASS) * v
        + get(co, a, n, EAST) * (v - from_east(v, step))
        + get(co, a, n, WEST) * (v - from_west(v, step))
        + get(co, a, n, SOUTH) * (v - get(v_ref, PAD + a + 1, n))
        + get(co, a, n, NORTH) * (v - get(v_ref, PAD + a - 1, n))
    )
    return v, out


def sweep(v_ref, to, co, b_ref, low, high, step):
    for a, n in chunks(low, high):
        v, out = operate(v_ref, co, a, n, step)
        rest = -out if b_ref is None else get(b_ref, a, n) - out
        put(to, PAD + a, v + rest * get(co, a, n, RATE))


def first_sweep(to, co, b_ref, low, high):
    for a, n in chunks(low, high):
        put(to, PAD + a, get(b_ref, a, n) * get(co, a, n, RATE))


def residual(v_ref, to, co, b_ref, low, high, step):
    for a, n in chunks(low, high):
        _, out = operate(v_ref, co, a, n, step)
        put(to, a, -out if b_ref is None else get(b_ref, a, n) - out)


def block_sum(fine, a, n, step, *at):
    return pair_sum(get_strided(fine, 2 * a, n, *at) + get_strided(fine, 2 * a + 1, n, *at), step)


def restrict(fine, to, low, high, step):
    for a, n in chunks(low // 2, high // 2):
        put(to, a, block_sum(fine, a, n, step))


def prolong(coarse, base, to, low, high):
    for a, n in chunks(low // 2, high // 2):
        value = get(coarse, PAD + a, n)
        for p in range(2):
            for h in range(to.shape[0]):
                part = value[:, 128 * h : 128 * h + 128]
                rows = pl.ds(PAD + 2 * a + p, n, stride=2)
                to[h, rows, :] = part if base is None else base[h, rows, :] + part


def diagonal(co, a, n):
    total = get(co, a, n, MASS)
    for k in (EAST, WEST, SOUTH, NORTH):
        total = total + get(co, a, n, k)
    return total


def coarsen(fine, to, rows, step):
    for a, n in chunks(0, rows):
        put(to, a, block_sum(fine, a, n, step, MASS), MASS)
        east = get_strided(fine, 2 * a, n, EAST) + get_strided(fine, 2 * a + 1, n, EAST)
        put(to, a, jnp.where(first_of_pair(east, step), from_east(east, step), east), EAST)
        west = get_strided(fine, 2 * a, n, WEST) + get_strided(fine, 2 * a + 1, n, WEST)
        put(to, a, jnp.where(first_of_pair(west, step), west, from_west(west, step)), WEST)
        put(to, a, pair_sum(get_strided(fine, 2 * a + 1, n, SOUTH), step), SOUTH)
        put(to, a, pair_sum(get_strided(fine, 2 * a, n, NORTH), step), NORTH)


def set_rate(co, rows):
    for a, n in chunks(0, rows):
        d = diagonal(co, a, n)
        put(co, a, RELAX / jnp.where(d > 0, d, 1.0), RATE)


STATE = (208, 112, 64, 96, 48, 192)
STATE_ROWS = sum(STATE)


def state_of(ref):
    starts = [sum(STATE[:k]) for k in range(6)]
    return [ref.at[:, pl.ds(start, count), :] for start, count in zip(starts, STATE)]


def field(*shape):
    return jax.ShapeDtypeStruct(shape, F32)


def scratch(*shape):
    return pltpu.VMEM(shape, F32)


def call(body, outs, scratches, *args, at=pltpu.VMEM, cycles=1000, room=12):
    vmem = pl.BlockSpec(memory_space=pltpu.VMEM)
    return pl.pallas_call(
        body,
        out_shape=outs,
        in_specs=[pl.BlockSpec(memory_space=at)] * len(args),
        out_specs=[vmem] * len(outs) if isinstance(outs, tuple) else vmem,
        scratch_shapes=scratches,
        cost_estimate=pl.CostEstimate(flops=2000 * cycles, bytes_accessed=2000 * cycles, transcendentals=0),
        compiler_params=pltpu.CompilerParams(vmem_limit_bytes=room * 1024 * 1024),
    )(*args)


def prepare(*refs):
    sources, (own, first, second), temps, arrived = refs[:5], refs[5:8], refs[8:13], refs[13]
    copies = [pltpu.make_async_copy(sources[k], temps[k], arrived.at[k]) for k in range(5)]
    for copy in copies:
        copy.start()
    for copy in copies:
        copy.wait()
    right, previous, east, south, mask = temps
    wet = mask[...] > 0
    own[0] = jnp.where(wet, east[...], 0.0)
    own[1] = jnp.where(wet, south[...], 0.0)
    own[2] = jnp.where(wet, right[...], previous[...])
    own[3] = previous[...]
    low = lanes((64, 128)) < 64
    even = lax.rem(lax.axis_index("x"), 2) == 0
    for k in range(2):
        a, b = own[2 * k], pltpu.roll(own[2 * k + 1], 64, 1)
        to_east, to_west = jnp.where(low, b, a), jnp.where(low, a, b)
        first[k] = jnp.where(even, to_east, to_west)
        second[k] = jnp.where(even, to_west, to_east)


def widen(own, first, second, out):
    low = lanes((64, 128)) < 64
    even = lax.rem(lax.axis_index("x"), 2) == 0
    for k in range(2):
        e = jnp.where(even, first[k], second[k])
        w = jnp.where(even, second[k], first[k])
        out[2 * k] = own[2 * k]
        out[2 * k + 1] = own[2 * k + 1]
        out[4 + 2 * k] = jnp.where(low, e, w)
        out[5 + 2 * k] = jnp.where(low, pltpu.roll(e, 64, 1), pltpu.roll(w, 64, 1))


def descend(v1_ref, v2_ref, b1_ref, b2_ref, b3_ref, co, rest, temp, ranges):
    (l0, h0), (l1, h1), (l2, h2), (l3, h3) = ranges
    restrict(rest[0], b1_ref, l0, h0, 1)
    first_sweep(temp[1], co[1], b1_ref, l1, h1)
    sweep(temp[1], v1_ref, co[1], b1_ref, l1, h1, 2)
    residual(v1_ref, rest[1], co[1], b1_ref, l1, h1, 2)
    restrict(rest[1], b2_ref, l1, h1, 2)
    first_sweep(temp[2], co[2], b2_ref, l2, h2)
    sweep(temp[2], v2_ref, co[2], b2_ref, l2, h2, 4)
    residual(v2_ref, rest[2], co[2], b2_ref, l2, h2, 4)
    restrict(rest[2], b3_ref, l3, h3, 4)


def first_leg(own, first, second, co0, co1, co2, state, co3, packed, *temps):
    v0, v1, v2, b1, b2, b0 = state_of(state)
    wet_ref, south_ref, t0, t1, t2, r0, r1, r2, b3 = temps
    even = lax.rem(lax.axis_index("grp"), 2) == 0

    def window(k, a, n):
        part, o = a // 64, a % 64
        if part == 1:
            return jnp.concatenate([own[k, o : o + n, :], own[4 + k, o : o + n, :]], axis=1)
        up, down = (second, first) if part == 0 else (first, second)
        halves = [jnp.where(even, up[h, o : o + n, :], down[h, o : o + n, :]) for h in (k, 4 + k)]
        return jnp.concatenate(halves, axis=1)

    for a, n in chunks(0, 192):
        put(wet_ref, PAD + a, jnp.where(window(0, a, n) > 0, 1.0, 0.0))
        put(v0, PAD + a, window(3, a, n))
        put(b0, a, window(2, a, n))
    for a, n in chunks(0, 192):
        wet = get(wet_ref, PAD + a, n)
        east = window(0, a, n) * from_east(wet, 1)
        south = window(1, a, n) * get(wet_ref, PAD + a + 1, n)
        put(co0, a, east, EAST)
        put(co0, a, from_west(east, 1), WEST)
        put(co0, a, south, SOUTH)
        put(south_ref, PAD + a, south)
        put(co0, a, wet * WET_MASS + (1.0 - wet), MASS)
    for a, n in chunks(0, 192):
        put(co0, a, get(south_ref, PAD + a - 1, n), NORTH)
    set_rate(co0, 192)
    coarsen(co0, co1, 96, 1)
    set_rate(co1, 96)
    coarsen(co1, co2, 48, 2)
    set_rate(co2, 48)
    coarsen(co2, co3, 24, 4)
    set_rate(co3, 24)
    sweep(v0, t0, co0, b0, 0, 192, 1)
    sweep(t0, v0, co0, b0, 0, 192, 1)
    residual(v0, r0, co0, b0, 0, 192, 1)
    descend(
        v1, v2, b1, b2, b3, (co0, co1, co2), (r0, r1, r2), (t0, t1, t2), ((0, 192), (0, 96), (0, 48), (16, 32))
    )
    slot = lanes((8, 128)) & 7
    values = (
        b3[0, 8:16, :],
        co3[MASS, 0, 8:16, :],
        co3[EAST, 0, 8:16, :],
        co3[SOUTH, 0, 8:16, :],
        diagonal(co3, 8, 8)[:, :128],
    )
    out = jnp.zeros((8, 128), F32)
    for k, value in enumerate(values):
        out = jnp.where(slot == k, value, out)
    packed[...] = out


def fan(own, crossed, responded, out):
    full = jnp.where((lanes((8, 128)) & 7) == 5, responded[...], own[...])
    for k in range(out.shape[0]):
        out[k, 0] = full
        out[k, 1] = crossed[...]


def ascend(coarse, bases, sources, to, temp, co):
    ranges = ((32, 160), (8, 88), (0, 48))
    for level in (2, 1, 0):
        low, high = ranges[level]
        step = 1 << level
        prolong(coarse, bases[level], to[level], low, high)
        sweep(to[level], temp[level], co[level], sources[level], low, high, step)
        sweep(temp[level], to[level], co[level], sources[level], low, high, step)
        coarse = to[level]


def second_descent(start, source, kept, rest, temp, co):
    v0, v1, v2, b1, b2, b3 = kept
    sweep(start, temp[0], co[0], source, 32, 160, 1)
    sweep(temp[0], v0, co[0], source, 32, 160, 1)
    residual(v0, rest[0], co[0], source, 32, 160, 1)
    descend(v1, v2, b1, b2, b3, co, rest, temp, ((32, 160), (16, 80), (8, 40), (16, 32)))


def response(co0, co1, co2, co3, state, packed, *temps):
    v0, v1, v2, b1, b2, _ = state_of(state)
    t0, s0, t1, s1, t2, s2, v3, s3, r0, r1, r2, b3 = temps
    put(v3, PAD, jnp.ones((24, 256), F32))
    sweep(v3, s3, co3, None, 0, 24, 8)
    sweep(s3, v3, co3, None, 0, 24, 8)
    none, co = (None, None, None), (co0, co1, co2)
    ascend(v3, none, none, (t0, t1, t2), (s0, s1, s2), co)
    second_descent(t0, None, (v0, v1, v2, b1, b2, b3), (r0, r1, r2), (s0, s1, s2), co)
    packed[...] = b3[0, 8:16, :]


def neighbours():
    group, x = lax.axis_index("grp"), lax.axis_index("x")
    inner_west, inner_east = x > 0, x < 3
    return group, x, inner_west, inner_east, jnp.where(inner_west, x - 1, 3), jnp.where(inner_east, x + 1, 0)


def spread(x, slot):
    y = jnp.where((lanes(x.shape) & 7) == slot, x, 0.0)
    for step in (1, 2, 4):
        y = pair_sum(y, step)
    return y


def inner_part(wide, to):
    to[0, pl.ds(PAD, 24), :] = wide[1, pl.ds(PAD + 8, 24), :]
    low = lanes((24, 128)) < 64
    to[1, pl.ds(PAD, 24), :] = jnp.where(low, wide[2, pl.ds(PAD + 8, 24), :], wide[0, pl.ds(PAD + 8, 24), :])


def solve_coarse(b3, b4, co3, co4, v3, s3, v4, s4, rest, shift):
    first_sweep(s3, co3, b3, 0, 40)
    sweep(s3, v3, co3, b3, 0, 40, 8)
    residual(v3, rest, co3, b3, 0, 40, 8)
    restrict(rest, b4, 0, 48, 8)
    first_sweep(s4, co4, b4, 0, 24)
    sweep(s4, v4, co4, b4, 0, 24, 16)
    sweep(v4, s4, co4, b4, 0, 24, 16)
    sweep(s4, v4, co4, b4, 0, 24, 16)
    if shift is not None:
        put(v4, PAD, get(v4, PAD, 24) + shift)
    prolong(v4, v3, v3, 0, 40)
    sweep(v3, s3, co3, b3, 0, 40, 8)
    sweep(s3, v3, co3, b3, 0, 40, 8)


def second_leg(gathered, responded, co0, co1, co2, before, co3, co4, after, packed, *temps):
    v0, v1, v2, b1, b2, b0 = state_of(before)
    v0a, v1a, v2a, b1a, b2a, _ = state_of(after)
    (t0, s0, t1, s1, t2, s2, r0, r1, r2, e3, bn, b3, b4, v3, s3, w3, v4, s4, r3, south_ref) = temps
    group, own, inner_west, inner_east, at_west, at_east = neighbours()
    at_west = 2 * at_west + jnp.where(inner_west, 0, 1)
    at_east = 2 * at_east + jnp.where(inner_east, 0, 1)
    for t in range(5):
        at = group + (t - 2)
        valid = jnp.logical_and(at >= 0, at < 8).astype(F32)
        at = 8 * jnp.clip(at, 0, 7)
        x = jnp.concatenate([gathered[at + k] for k in (at_west, 2 * own, at_east)], axis=1) * valid
        row = 8 * t
        put(b3, row, spread(x, 0))
        put(co3, row, spread(x, 1), MASS)
        east = spread(x, 2)
        put(co3, row, east, EAST)
        put(co3, row, from_west(east, 8), WEST)
        south = spread(x, 3)
        put(co3, row, south, SOUTH)
        put(south_ref, PAD + row, south)
        d = spread(x, 4)
        put(co3, row, RELAX / jnp.where(d > 0, d, 1.0), RATE)
    for a, n in chunks(0, 40):
        put(co3, a, get(south_ref, PAD + a - 1, n), NORTH)
    coarsen(co3, co4, 20, 8)
    set_rate(co4, 24)

    put(v4, PAD, jnp.ones((24, 384), F32))
    for here, there in ((v4, s4), (s4, v4), (v4, s4), (s4, v4)):
        sweep(here, there, co4, None, 0, 24, 16)
    prolong(v4, None, w3, 0, 40)
    sweep(w3, s3, co3, None, 0, 40, 8)
    sweep(s3, w3, co3, None, 0, 40, 8)
    weight = w3[1, pl.ds(PAD + 16, 8), :]

    solve_coarse(b3, b4, co3, co4, v3, s3, v4, s4, r3, None)
    inner_part(v3, e3)
    co = (co0, co1, co2)
    ascend(e3, (v0, v1, v2), (b0, b1, b2), (t0, t1, t2), (s0, s1, s2), co)
    second_descent(t0, b0, (v0a, v1a, v2a, b1a, b2a, bn), (r0, r1, r2), (s0, s1, s2), co)
    result = bn[0, 8:16, :]
    place = lanes((8, 128))
    slot = place & 7
    out = jnp.where(slot == 0, result, jnp.where(slot == 1, responded[...], 0.0))
    mass = co3[MASS, 1, 16:24, :]
    sums = (mass, weight * b3[1, 16:24, :], weight * result, weight * responded[...])
    for k, value in enumerate(sums):
        once = jnp.where(slot == 0, value, 0.0)
        total = jnp.sum(jnp.sum(once, axis=0, keepdims=True), axis=1, keepdims=True)
        out = jnp.where(place == 8 * k + 6, total, out)
    for z in range(packed.shape[0]):
        packed[z] = out


def relay(gathered, out):
    z = lax.axis_index("z")
    last = gathered.shape[0] - 1
    own = gathered[z]
    before = gathered[jnp.maximum(z - 1, 0)]
    after = gathered[jnp.minimum(z + 1, last)]
    total = gathered[0]
    for k in range(1, last + 1):
        total = total + gathered[k]
    slot = lanes((8, 128)) & 7
    value = jnp.where(slot < 2, own, jnp.where(slot < 4, pltpu.roll(before, 2, 1), pltpu.roll(after, 4, 1)))
    value = jnp.where(slot < 6, value, total)
    for k in range(out.shape[0]):
        out[k] = value


def third_leg(gathered, co0, co1, co2, before, co3, co4, after, beside, *others):
    b0 = state_of(before)[5]
    v0a, v1a, v2a, b1a, b2a, _ = state_of(after)
    v0b, v1b, v2b, b1b, b2b, _ = state_of(beside)
    (surface, rest, *temps) = others
    (t0, s0, c0, t1, s1, c1, d1, t2, s2, c2, d2, e3, b3, b4, v3, s3, v4, s4, r3) = temps
    total = gathered[0]
    for k in range(1, gathered.shape[0]):
        total = total + gathered[k]
    place = lanes((1, 128))
    mass, sum1, sum2a, sum2b = (
        jnp.sum(jnp.where(place == 8 * k + 6, total[:1], 0.0), axis=1, keepdims=True) for k in range(4)
    )
    shift1 = RELAX * sum1 / mass
    shift2 = RELAX * (sum2a + shift1 * sum2b) / mass

    group, x, inner_west, inner_east, at_west, at_east = neighbours()
    for t in range(5):
        g = 4 * jnp.clip(group + (t - 2), 0, 7)
        w, o, e = gathered[g + at_west], gathered[g + x], gathered[g + at_east]
        w = jnp.where(inner_west, w, pltpu.roll(w, 126, 1))
        e = jnp.where(inner_east, e, pltpu.roll(e, 124, 1))
        both = jnp.concatenate([w, o, e], axis=1)
        put(b3, 8 * t, spread(both + shift1 * from_east(both, 1), 0))
    solve_coarse(b3, b4, co3, co4, v3, s3, v4, s4, r3, shift2)
    inner_part(v3, e3)

    def combine(to, first, second, offset, low, high):
        for a, n in chunks(offset + low, offset + high):
            put(to, a, get(first, a, n) + shift1 * get(second, a, n))

    combine(c2, v2a, v2b, PAD, 8, 40)
    combine(d2, b2a, b2b, 0, 8, 40)
    combine(c1, v1a, v1b, PAD, 24, 72)
    combine(d1, b1a, b1b, 0, 24, 72)
    combine(c0, v0a, v0b, PAD, 56, 136)
    prolong(e3, c2, t2, 8, 40)
    sweep(t2, s2, co2, d2, 8, 40, 4)
    sweep(s2, t2, co2, d2, 8, 40, 4)
    prolong(t2, c1, t1, 24, 72)
    sweep(t1, s1, co1, d1, 24, 72, 2)
    sweep(s1, t1, co1, d1, 24, 72, 2)
    prolong(t1, c0, t0, 56, 136)
    sweep(t0, s0, co0, b0, 56, 136, 1)
    sweep(s0, t0, co0, b0, 56, 136, 1)
    surface[...] = t0[0, pl.ds(PAD + 64, 64), :]
    for a, n in chunks(64, 128):
        _, out = operate(t0, co0, a, n, 1)
        rest[a - 64 : a - 64 + n, :] = b0[0, a : a + n, :] - out[:, :128]


def swaps(start, count):
    low = range(start, count - 1, 2)
    return [(i, i + 1) for i in low] + [(i + 1, i) for i in low]


def shards(right_side, previous, east_face, south_face, wet_mask):
    dev = ("z", "x")
    own, first, second = call(
        prepare,
        (scratch(4, 64, 128), scratch(2, 64, 128), scratch(2, 64, 128)),
        [*[scratch(64, 128)] * 4, pltpu.VMEM((64, 128), jnp.int32), pltpu.SemaphoreType.DMA((5,))],
        right_side,
        previous,
        east_face,
        south_face,
        wet_mask,
        at=pltpu.HBM,
        room=60,
    )
    first = lax.ppermute(first, dev, swaps(0, 64))
    second = lax.ppermute(second, dev, swaps(1, 64))
    own = call(widen, field(8, 64, 128), [], own, first, second)
    first = lax.ppermute(own, "grp", swaps(0, 8))
    second = lax.ppermute(own, "grp", swaps(1, 8))

    def rows(count, planes=2):
        return field(planes, count, 128)

    def shifted(count, planes=2):
        return field(planes, count + 2 * PAD, 128)

    def as_scratch(*fields):
        return [scratch(*f.shape) for f in fields]

    co = [field(6, 2, count, 128) for count in (192, 96, 48, 24)]
    fine = [shifted(count) for count in (192, 96, 48)]
    sources = [rows(count) for count in (192, 96, 48)]
    state = rows(STATE_ROWS)
    *kept, near, packed = call(
        first_leg,
        (*co[:3], state, co[3], field(8, 128)),
        as_scratch(fine[0], fine[0], *fine, *sources, rows(24)),
        own,
        first,
        second,
    )
    crossings = [(4 * z + 3, 4 * z + 7) for z in range(15)] + [(4 * z + 4, 4 * z) for z in range(15)]
    crossed = lax.ppermute(packed, dev, crossings)
    beside, responded = call(
        response,
        (state, field(8, 128)),
        as_scratch(*[f for f in fine for _ in range(2)], shifted(24), shifted(24), *sources, rows(24)),
        *kept[:3],
        near,
        cycles=3000,
    )
    gathered = call(fan, field(32, 2, 8, 128), [], packed, crossed, responded)
    gathered = lax.all_to_all(gathered, ("grp", "x"), 0, 0, tiled=True).reshape(64, 8, 128)
    coarse = [shifted(40, 3), shifted(40, 3), shifted(40, 3), shifted(24, 3), shifted(24, 3)]
    *second, packed = call(
        second_leg,
        (field(6, 3, 40, 128), field(6, 3, 24, 128), state, field(16, 8, 128)),
        as_scratch(
            *[f for f in fine for _ in range(2)],
            *sources,
            shifted(24),
            rows(24),
            rows(40, 3),
            rows(24, 3),
            *coarse,
            rows(48, 3),
            shifted(40, 3),
        ),
        gathered,
        responded,
        *kept,
    )
    gathered = lax.all_to_all(packed, "z", 0, 0, tiled=True)
    gathered = call(relay, field(32, 8, 128), [], gathered)
    gathered = lax.all_to_all(gathered, ("grp", "x"), 0, 0, tiled=True)
    surface, rest = call(
        third_leg,
        (field(64, 128), field(64, 128)),
        as_scratch(
            *[shifted(192)] * 3,
            *[shifted(96)] * 3,
            rows(96),
            *[shifted(48)] * 3,
            rows(48),
            shifted(24),
            rows(40, 3),
            rows(24, 3),
            shifted(40, 3),
            shifted(40, 3),
            shifted(24, 3),
            shifted(24, 3),
            rows(48, 3),
        ),
        gathered,
        *kept,
        *second,
        beside,
    )
    return surface, rest


def solution(mesh):
    split = Mesh(mesh.devices.reshape(8, 16, 4), ("grp", "z", "x"))
    placed = P("grp", ("z", "x"))
    return jax.shard_map(shards, mesh=split, in_specs=(placed,) * 5, out_specs=(placed,) * 2, check_vma=False)
```

```python
import jax
import jax.numpy as jnp
from jax import lax
from jax.experimental import pallas as pl
from jax.experimental.pallas import tpu as pltpu
from jax.sharding import Mesh
from jax.sharding import PartitionSpec as P

F32 = jnp.float32
RELAX = 0.8
WET_MASS = 2e-05
PAD = 8
CHUNK = 16
EAST, WEST, SOUTH, NORTH, MASS, RATE = range(6)


def lanes(shape):
    return lax.broadcasted_iota(jnp.int32, shape, len(shape) - 1)


def from_east(x, step):
    return pltpu.roll(x, x.shape[1] - step, 1)


def from_west(x, step):
    return pltpu.roll(x, step, 1)


def first_of_pair(x, step):
    return (lanes(x.shape) & step) == 0


def pair_sum(x, step):
    return x + jnp.where(first_of_pair(x, step), from_east(x, step), from_west(x, step))


def get(ref, start, count, *at):
    return jnp.concatenate([ref[(*at, h, pl.ds(start, count), slice(None))] for h in range(ref.shape[len(at)])], axis=1)


def get_strided(ref, start, count, *at):
    return jnp.concatenate(
        [ref[(*at, h, pl.ds(start, count, stride=2), slice(None))] for h in range(ref.shape[len(at)])], axis=1
    )


def put(ref, start, value, *at):
    for h in range(ref.shape[len(at)]):
        ref[(*at, h, pl.ds(start, value.shape[0]), slice(None))] = value[:, 128 * h : 128 * h + 128]


def chunks(low, high, size=CHUNK):
    return [(a, min(size, high - a)) for a in range(low, high, size)]


def operate(v_ref, co, a, n, step):
    v = get(v_ref, PAD + a, n)
    out = (
        get(co, a, n, MASS) * v
        + get(co, a, n, EAST) * (v - from_east(v, step))
        + get(co, a, n, WEST) * (v - from_west(v, step))
        + get(co, a, n, SOUTH) * (v - get(v_ref, PAD + a + 1, n))
        + get(co, a, n, NORTH) * (v - get(v_ref, PAD + a - 1, n))
    )
    return v, out


def sweep(v_ref, to, co, b_ref, low, high, step):
    for a, n in chunks(low, high):
        v, out = operate(v_ref, co, a, n, step)
        rest = -out if b_ref is None else get(b_ref, a, n) - out
        put(to, PAD + a, v + rest * get(co, a, n, RATE))


def first_sweep(to, co, b_ref, low, high):
    for a, n in chunks(low, high):
        put(to, PAD + a, get(b_ref, a, n) * get(co, a, n, RATE))


def residual(v_ref, to, co, b_ref, low, high, step):
    for a, n in chunks(low, high):
        _, out = operate(v_ref, co, a, n, step)
        put(to, a, -out if b_ref is None else get(b_ref, a, n) - out)


def block_sum(fine, a, n, step, *at):
    return pair_sum(get_strided(fine, 2 * a, n, *at) + get_strided(fine, 2 * a + 1, n, *at), step)


def restrict(fine, to, low, high, step):
    for a, n in chunks(low // 2, high // 2):
        put(to, a, block_sum(fine, a, n, step))


def prolong(coarse, base, to, low, high):
    for a, n in chunks(low // 2, high // 2):
        value = get(coarse, PAD + a, n)
        for p in range(2):
            for h in range(to.shape[0]):
                part = value[:, 128 * h : 128 * h + 128]
                rows = pl.ds(PAD + 2 * a + p, n, stride=2)
                to[h, rows, :] = part if base is None else base[h, rows, :] + part


def diagonal(co, a, n):
    total = get(co, a, n, MASS)
    for k in (EAST, WEST, SOUTH, NORTH):
        total = total + get(co, a, n, k)
    return total


def coarsen(fine, to, rows, step):
    for a, n in chunks(0, rows):
        put(to, a, block_sum(fine, a, n, step, MASS), MASS)
        east = get_strided(fine, 2 * a, n, EAST) + get_strided(fine, 2 * a + 1, n, EAST)
        put(to, a, jnp.where(first_of_pair(east, step), from_east(east, step), east), EAST)
        west = get_strided(fine, 2 * a, n, WEST) + get_strided(fine, 2 * a + 1, n, WEST)
        put(to, a, jnp.where(first_of_pair(west, step), west, from_west(west, step)), WEST)
        put(to, a, pair_sum(get_strided(fine, 2 * a + 1, n, SOUTH), step), SOUTH)
        put(to, a, pair_sum(get_strided(fine, 2 * a, n, NORTH), step), NORTH)


def set_rate(co, rows):
    for a, n in chunks(0, rows):
        d = diagonal(co, a, n)
        put(co, a, RELAX / jnp.where(d > 0, d, 1.0), RATE)


STATE = (208, 112, 64, 96, 48, 192)
STATE_ROWS = sum(STATE)


def state_of(ref):
    starts = [sum(STATE[:k]) for k in range(6)]
    return [ref.at[:, pl.ds(start, count), :] for start, count in zip(starts, STATE)]


def field(*shape):
    return jax.ShapeDtypeStruct(shape, F32)


def scratch(*shape):
    return pltpu.VMEM(shape, F32)


def call(body, outs, scratches, *args, at=pltpu.VMEM, cycles=1000, room=12):
    vmem = pl.BlockSpec(memory_space=pltpu.VMEM)
    return pl.pallas_call(
        body,
        out_shape=outs,
        in_specs=[pl.BlockSpec(memory_space=at)] * len(args),
        out_specs=[vmem] * len(outs) if isinstance(outs, tuple) else vmem,
        scratch_shapes=scratches,
        cost_estimate=pl.CostEstimate(flops=2000 * cycles, bytes_accessed=2000 * cycles, transcendentals=0),
        compiler_params=pltpu.CompilerParams(vmem_limit_bytes=room * 1024 * 1024),
    )(*args)


def prepare(*refs):
    sources, (own, first, second), temps, arrived = refs[:5], refs[5:8], refs[8:13], refs[13]
    copies = [pltpu.make_async_copy(sources[k], temps[k], arrived.at[k]) for k in range(5)]
    for copy in copies:
        copy.start()
    for copy in copies:
        copy.wait()
    right, previous, east, south, mask = temps
    wet = mask[...] > 0
    own[0] = jnp.where(wet, east[...], 0.0)
    own[1] = jnp.where(wet, south[...], 0.0)
    own[2] = jnp.where(wet, right[...], previous[...])
    own[3] = previous[...]
    low = lanes((64, 128)) < 64
    even = lax.rem(lax.axis_index("x"), 2) == 0
    for k in range(2):
        a, b = own[2 * k], pltpu.roll(own[2 * k + 1], 64, 1)
        to_east, to_west = jnp.where(low, b, a), jnp.where(low, a, b)
        first[k] = jnp.where(even, to_east, to_west)
        second[k] = jnp.where(even, to_west, to_east)


def widen(own, second, first, out):
    low = lanes((64, 128)) < 64
    even = lax.rem(lax.axis_index("x"), 2) == 0
    for k in range(2):
        e = jnp.where(even, first[k], second[k])
        w = jnp.where(even, second[k], first[k])
        out[2 * k] = own[2 * k]
        out[2 * k + 1] = own[2 * k + 1]
        out[4 + 2 * k] = jnp.where(low, e, w)
        out[5 + 2 * k] = jnp.where(low, pltpu.roll(e, 64, 1), pltpu.roll(w, 64, 1))


def descend(v1_ref, v2_ref, b1_ref, b2_ref, b3_ref, co, rest, temp, ranges):
    (l0, h0), (l1, h1), (l2, h2), (l3, h3) = ranges
    restrict(rest[0], b1_ref, l0, h0, 1)
    first_sweep(temp[1], co[1], b1_ref, l1, h1)
    sweep(temp[1], v1_ref, co[1], b1_ref, l1, h1, 2)
    residual(v1_ref, rest[1], co[1], b1_ref, l1, h1, 2)
    restrict(rest[1], b2_ref, l1, h1, 2)
    first_sweep(temp[2], co[2], b2_ref, l2, h2)
    sweep(temp[2], v2_ref, co[2], b2_ref, l2, h2, 4)
    residual(v2_ref, rest[2], co[2], b2_ref, l2, h2, 4)
    restrict(rest[2], b3_ref, l3, h3, 4)


def first_leg(own, first, second, co0, co1, co2, state, co3, packed, *temps):
    v0, v1, v2, b1, b2, b0 = state_of(state)
    wet_ref, south_ref, t0, t1, t2, r0, r1, r2, b3 = temps
    even = lax.rem(lax.axis_index("grp"), 2) == 0

    def window(k, a, n):
        part, o = a // 64, a % 64
        if part == 1:
            return jnp.concatenate([own[k, o : o + n, :], own[4 + k, o : o + n, :]], axis=1)
        up, down = (second, first) if part == 0 else (first, second)
        halves = [jnp.where(even, up[h, o : o + n, :], down[h, o : o + n, :]) for h in (k, 4 + k)]
        return jnp.concatenate(halves, axis=1)

    for a, n in chunks(0, 192):
        put(wet_ref, PAD + a, jnp.where(window(0, a, n) > 0, 1.0, 0.0))
        put(v0, PAD + a, window(3, a, n))
        put(b0, a, window(2, a, n))
    for a, n in chunks(0, 192):
        wet = get(wet_ref, PAD + a, n)
        east = window(0, a, n) * from_east(wet, 1)
        south = window(1, a, n) * get(wet_ref, PAD + a + 1, n)
        put(co0, a, east, EAST)
        put(co0, a, from_west(east, 1), WEST)
        put(co0, a, south, SOUTH)
        put(south_ref, PAD + a, south)
        put(co0, a, wet * WET_MASS + (1.0 - wet), MASS)
    for a, n in chunks(0, 192):
        put(co0, a, get(south_ref, PAD + a - 1, n), NORTH)
    set_rate(co0, 192)
    coarsen(co0, co1, 96, 1)
    set_rate(co1, 96)
    coarsen(co1, co2, 48, 2)
    set_rate(co2, 48)
    coarsen(co2, co3, 24, 4)
    set_rate(co3, 24)
    sweep(v0, t0, co0, b0, 0, 192, 1)
    sweep(t0, v0, co0, b0, 0, 192, 1)
    residual(v0, r0, co0, b0, 0, 192, 1)
    descend(
        v1, v2, b1, b2, b3, (co0, co1, co2), (r0, r1, r2), (t0, t1, t2), ((0, 192), (0, 96), (0, 48), (16, 32))
    )
    slot = lanes((8, 128)) & 7
    values = (
        b3[0, 8:16, :],
        co3[MASS, 0, 8:16, :],
        co3[EAST, 0, 8:16, :],
        co3[SOUTH, 0, 8:16, :],
        diagonal(co3, 8, 8)[:, :128],
    )
    out = jnp.zeros((8, 128), F32)
    for k, value in enumerate(values):
        out = jnp.where(slot == k, value, out)
    packed[...] = out


def fan(own, first, second, responded, out):
    even = lax.rem(lax.axis_index("x"), 2) == 0
    east = jnp.where(even, first[...], second[...])
    west = jnp.where(even, second[...], first[...])
    full = jnp.where((lanes((8, 128)) & 7) == 5, responded[...], own[...])
    for g in range(out.shape[0]):
        out[g, 0] = west
        out[g, 1] = full
        out[g, 2] = east


def ascend(coarse, bases, sources, to, temp, co):
    ranges = ((32, 160), (8, 88), (0, 48))
    for level in (2, 1, 0):
        low, high = ranges[level]
        step = 1 << level
        prolong(coarse, bases[level], to[level], low, high)
        sweep(to[level], temp[level], co[level], sources[level], low, high, step)
        sweep(temp[level], to[level], co[level], sources[level], low, high, step)
        coarse = to[level]


def second_descent(start, source, kept, rest, temp, co):
    v0, v1, v2, b1, b2, b3 = kept
    sweep(start, temp[0], co[0], source, 32, 160, 1)
    sweep(temp[0], v0, co[0], source, 32, 160, 1)
    residual(v0, rest[0], co[0], source, 32, 160, 1)
    descend(v1, v2, b1, b2, b3, co, rest, temp, ((32, 160), (16, 80), (8, 40), (16, 32)))


def response(co0, co1, co2, co3, state, packed, *temps):
    v0, v1, v2, b1, b2, _ = state_of(state)
    t0, s0, t1, s1, t2, s2, v3, s3, r0, r1, r2, b3 = temps
    put(v3, PAD, jnp.ones((24, 256), F32))
    sweep(v3, s3, co3, None, 0, 24, 8)
    sweep(s3, v3, co3, None, 0, 24, 8)
    none, co = (None, None, None), (co0, co1, co2)
    ascend(v3, none, none, (t0, t1, t2), (s0, s1, s2), co)
    second_descent(t0, None, (v0, v1, v2, b1, b2, b3), (r0, r1, r2), (s0, s1, s2), co)
    packed[...] = b3[0, 8:16, :]


def neighbours():
    group, x = lax.axis_index("grp"), lax.axis_index("x")
    inner_west, inner_east = x > 0, x < 3
    return group, x, inner_west, inner_east, jnp.where(inner_west, x - 1, 3), jnp.where(inner_east, x + 1, 0)


def spread(x, slot):
    y = jnp.where((lanes(x.shape) & 7) == slot, x, 0.0)
    for step in (1, 2, 4):
        y = pair_sum(y, step)
    return y


def inner_part(wide, to):
    to[0, pl.ds(PAD, 24), :] = wide[1, pl.ds(PAD + 8, 24), :]
    low = lanes((24, 128)) < 64
    to[1, pl.ds(PAD, 24), :] = jnp.where(low, wide[2, pl.ds(PAD + 8, 24), :], wide[0, pl.ds(PAD + 8, 24), :])


def solve_coarse(b3, b4, co3, co4, v3, s3, v4, s4, rest, shift):
    first_sweep(s3, co3, b3, 0, 40)
    sweep(s3, v3, co3, b3, 0, 40, 8)
    residual(v3, rest, co3, b3, 0, 40, 8)
    restrict(rest, b4, 0, 48, 8)
    first_sweep(s4, co4, b4, 0, 24)
    sweep(s4, v4, co4, b4, 0, 24, 16)
    sweep(v4, s4, co4, b4, 0, 24, 16)
    sweep(s4, v4, co4, b4, 0, 24, 16)
    if shift is not None:
        put(v4, PAD, get(v4, PAD, 24) + shift)
    prolong(v4, v3, v3, 0, 40)
    sweep(v3, s3, co3, b3, 0, 40, 8)
    sweep(s3, v3, co3, b3, 0, 40, 8)


def second_leg(gathered, responded, co0, co1, co2, before, co3, co4, after, packed, *temps):
    v0, v1, v2, b1, b2, b0 = state_of(before)
    v0a, v1a, v2a, b1a, b2a, _ = state_of(after)
    (t0, s0, t1, s1, t2, s2, r0, r1, r2, e3, bn, b3, b4, v3, s3, w3, v4, s4, r3, south_ref) = temps
    group = lax.axis_index("grp")
    for t in range(5):
        at = group + (t - 2)
        valid = jnp.logical_and(at >= 0, at < 8).astype(F32)
        at = jnp.clip(at, 0, 7)
        x = jnp.concatenate([gathered[at, k] for k in range(3)], axis=1) * valid
        row = 8 * t
        put(b3, row, spread(x, 0))
        put(co3, row, spread(x, 1), MASS)
        east = spread(x, 2)
        put(co3, row, east, EAST)
        put(co3, row, from_west(east, 8), WEST)
        south = spread(x, 3)
        put(co3, row, south, SOUTH)
        put(south_ref, PAD + row, south)
        d = spread(x, 4)
        put(co3, row, RELAX / jnp.where(d > 0, d, 1.0), RATE)
    for a, n in chunks(0, 40):
        put(co3, a, get(south_ref, PAD + a - 1, n), NORTH)
    coarsen(co3, co4, 20, 8)
    set_rate(co4, 24)

    put(v4, PAD, jnp.ones((24, 384), F32))
    for here, there in ((v4, s4), (s4, v4), (v4, s4), (s4, v4)):
        sweep(here, there, co4, None, 0, 24, 16)
    prolong(v4, None, w3, 0, 40)
    sweep(w3, s3, co3, None, 0, 40, 8)
    sweep(s3, w3, co3, None, 0, 40, 8)
    weight = w3[1, pl.ds(PAD + 16, 8), :]

    solve_coarse(b3, b4, co3, co4, v3, s3, v4, s4, r3, None)
    inner_part(v3, e3)
    co = (co0, co1, co2)
    ascend(e3, (v0, v1, v2), (b0, b1, b2), (t0, t1, t2), (s0, s1, s2), co)
    second_descent(t0, b0, (v0a, v1a, v2a, b1a, b2a, bn), (r0, r1, r2), (s0, s1, s2), co)
    result = bn[0, 8:16, :]
    place = lanes((8, 128))
    slot = place & 7
    out = jnp.where(slot == 0, result, jnp.where(slot == 1, responded[...], 0.0))
    mass = co3[MASS, 1, 16:24, :]
    sums = (mass, weight * b3[1, 16:24, :], weight * result, weight * responded[...])
    for k, value in enumerate(sums):
        once = jnp.where(slot == 0, value, 0.0)
        total = jnp.sum(jnp.sum(once, axis=0, keepdims=True), axis=1, keepdims=True)
        out = jnp.where(place == 8 * k + 6, total, out)
    for z in range(packed.shape[0]):
        packed[z] = out


def relay(gathered, out):
    z = lax.axis_index("z")
    last = gathered.shape[0] - 1
    own = gathered[z]
    before = gathered[jnp.maximum(z - 1, 0)]
    after = gathered[jnp.minimum(z + 1, last)]
    total = gathered[0]
    for k in range(1, last + 1):
        total = total + gathered[k]
    slot = lanes((8, 128)) & 7
    value = jnp.where(slot < 2, own, jnp.where(slot < 4, pltpu.roll(before, 2, 1), pltpu.roll(after, 4, 1)))
    value = jnp.where(slot < 6, value, total)
    for k in range(out.shape[0]):
        out[k] = value


def third_leg(gathered, co0, co1, co2, before, co3, co4, after, beside, *others):
    b0 = state_of(before)[5]
    v0a, v1a, v2a, b1a, b2a, _ = state_of(after)
    v0b, v1b, v2b, b1b, b2b, _ = state_of(beside)
    (surface, rest, *temps) = others
    (t0, s0, c0, t1, s1, c1, d1, t2, s2, c2, d2, e3, b3, b4, v3, s3, v4, s4, r3) = temps
    total = gathered[0]
    for k in range(1, gathered.shape[0]):
        total = total + gathered[k]
    place = lanes((1, 128))
    mass, sum1, sum2a, sum2b = (
        jnp.sum(jnp.where(place == 8 * k + 6, total[:1], 0.0), axis=1, keepdims=True) for k in range(4)
    )
    shift1 = RELAX * sum1 / mass
    shift2 = RELAX * (sum2a + shift1 * sum2b) / mass

    group, x, inner_west, inner_east, at_west, at_east = neighbours()
    for t in range(5):
        g = 4 * jnp.clip(group + (t - 2), 0, 7)
        w, o, e = gathered[g + at_west], gathered[g + x], gathered[g + at_east]
        w = jnp.where(inner_west, w, pltpu.roll(w, 126, 1))
        e = jnp.where(inner_east, e, pltpu.roll(e, 124, 1))
        both = jnp.concatenate([w, o, e], axis=1)
        put(b3, 8 * t, spread(both + shift1 * from_east(both, 1), 0))
    solve_coarse(b3, b4, co3, co4, v3, s3, v4, s4, r3, shift2)
    inner_part(v3, e3)

    def combine(to, first, second, offset, low, high):
        for a, n in chunks(offset + low, offset + high):
            put(to, a, get(first, a, n) + shift1 * get(second, a, n))

    combine(c2, v2a, v2b, PAD, 8, 40)
    combine(d2, b2a, b2b, 0, 8, 40)
    combine(c1, v1a, v1b, PAD, 24, 72)
    combine(d1, b1a, b1b, 0, 24, 72)
    combine(c0, v0a, v0b, PAD, 56, 136)
    prolong(e3, c2, t2, 8, 40)
    sweep(t2, s2, co2, d2, 8, 40, 4)
    sweep(s2, t2, co2, d2, 8, 40, 4)
    prolong(t2, c1, t1, 24, 72)
    sweep(t1, s1, co1, d1, 24, 72, 2)
    sweep(s1, t1, co1, d1, 24, 72, 2)
    prolong(t1, c0, t0, 56, 136)
    sweep(t0, s0, co0, b0, 56, 136, 1)
    sweep(s0, t0, co0, b0, 56, 136, 1)
    surface[...] = t0[0, pl.ds(PAD + 64, 64), :]
    for a, n in chunks(64, 128):
        _, out = operate(t0, co0, a, n, 1)
        rest[a - 64 : a - 64 + n, :] = b0[0, a : a + n, :] - out[:, :128]


def swaps(start, count):
    low = range(start, count - 1, 2)
    return [(i, i + 1) for i in low] + [(i + 1, i) for i in low]


def shards(right_side, previous, east_face, south_face, wet_mask):
    dev = ("z", "x")
    own, first, second = call(
        prepare,
        (scratch(4, 64, 128), scratch(2, 64, 128), scratch(2, 64, 128)),
        [*[scratch(64, 128)] * 4, pltpu.VMEM((64, 128), jnp.int32), pltpu.SemaphoreType.DMA((5,))],
        right_side,
        previous,
        east_face,
        south_face,
        wet_mask,
        at=pltpu.HBM,
        room=60,
    )
    first = lax.ppermute(first, dev, swaps(0, 64))
    second = lax.ppermute(second, dev, swaps(1, 64))
    own = call(widen, field(8, 64, 128), [], own, second, first)
    first = lax.ppermute(own, "grp", swaps(0, 8))
    second = lax.ppermute(own, "grp", swaps(1, 8))

    def rows(count, planes=2):
        return field(planes, count, 128)

    def shifted(count, planes=2):
        return field(planes, count + 2 * PAD, 128)

    def as_scratch(*fields):
        return [scratch(*f.shape) for f in fields]

    co = [field(6, 2, count, 128) for count in (192, 96, 48, 24)]
    fine = [shifted(count) for count in (192, 96, 48)]
    sources = [rows(count) for count in (192, 96, 48)]
    state = rows(STATE_ROWS)
    *kept, near, packed = call(
        first_leg,
        (*co[:3], state, co[3], field(8, 128)),
        as_scratch(fine[0], fine[0], *fine, *sources, rows(24)),
        own,
        first,
        second,
    )
    first = lax.ppermute(packed, dev, swaps(0, 64))
    second = lax.ppermute(packed, dev, swaps(1, 64))
    beside, responded = call(
        response,
        (state, field(8, 128)),
        as_scratch(*[f for f in fine for _ in range(2)], shifted(24), shifted(24), *sources, rows(24)),
        *kept[:3],
        near,
        cycles=3000,
    )
    gathered = call(fan, field(8, 3, 8, 128), [], packed, first, second, responded)
    gathered = lax.all_to_all(gathered, "grp", 0, 0, tiled=True)
    coarse = [shifted(40, 3), shifted(40, 3), shifted(40, 3), shifted(24, 3), shifted(24, 3)]
    *second, packed = call(
        second_leg,
        (field(6, 3, 40, 128), field(6, 3, 24, 128), state, field(16, 8, 128)),
        as_scratch(
            *[f for f in fine for _ in range(2)],
            *sources,
            shifted(24),
            rows(24),
            rows(40, 3),
            rows(24, 3),
            *coarse,
            rows(48, 3),
            shifted(40, 3),
        ),
        gathered,
        responded,
        *kept,
    )
    gathered = lax.all_to_all(packed, "z", 0, 0, tiled=True)
    gathered = call(relay, field(32, 8, 128), [], gathered)
    gathered = lax.all_to_all(gathered, ("grp", "x"), 0, 0, tiled=True)
    surface, rest = call(
        third_leg,
        (field(64, 128), field(64, 128)),
        as_scratch(
            *[shifted(192)] * 3,
            *[shifted(96)] * 3,
            rows(96),
            *[shifted(48)] * 3,
            rows(48),
            shifted(24),
            rows(40, 3),
            rows(24, 3),
            shifted(40, 3),
            shifted(40, 3),
            shifted(24, 3),
            shifted(24, 3),
            rows(48, 3),
        ),
        gathered,
        *kept,
        *second,
        beside,
    )
    return surface, rest


def solution(mesh):
    split = Mesh(mesh.devices.reshape(8, 16, 4), ("grp", "z", "x"))
    placed = P("grp", ("z", "x"))
    return jax.shard_map(shards, mesh=split, in_specs=(placed,) * 5, out_specs=(placed,) * 2, check_vma=False)
```

```python
import jax
import jax.numpy as jnp
from jax import lax
from jax.experimental import pallas as pl
from jax.experimental.pallas import tpu as pltpu
from jax.sharding import Mesh
from jax.sharding import PartitionSpec as P

F32 = jnp.float32
RELAX = 0.8
WET_MASS = 2e-05
PAD = 8
CHUNK = 16
EAST, WEST, SOUTH, NORTH, MASS, RATE = range(6)


def lanes(shape):
    return lax.broadcasted_iota(jnp.int32, shape, len(shape) - 1)


def from_east(x, step):
    return pltpu.roll(x, x.shape[1] - step, 1)


def from_west(x, step):
    return pltpu.roll(x, step, 1)


def first_of_pair(x, step):
    return (lanes(x.shape) & step) == 0


def pair_sum(x, step):
    return x + jnp.where(first_of_pair(x, step), from_east(x, step), from_west(x, step))


def get(ref, start, count, *at):
    return jnp.concatenate([ref[(*at, h, pl.ds(start, count), slice(None))] for h in range(ref.shape[len(at)])], axis=1)


def get_strided(ref, start, count, *at):
    return jnp.concatenate(
        [ref[(*at, h, pl.ds(start, count, stride=2), slice(None))] for h in range(ref.shape[len(at)])], axis=1
    )


def put(ref, start, value, *at):
    for h in range(ref.shape[len(at)]):
        ref[(*at, h, pl.ds(start, value.shape[0]), slice(None))] = value[:, 128 * h : 128 * h + 128]


def chunks(low, high, size=CHUNK):
    return [(a, min(size, high - a)) for a in range(low, high, size)]


def operate(v_ref, co, a, n, step):
    v = get(v_ref, PAD + a, n)
    out = (
        get(co, a, n, MASS) * v
        + get(co, a, n, EAST) * (v - from_east(v, step))
        + get(co, a, n, WEST) * (v - from_west(v, step))
        + get(co, a, n, SOUTH) * (v - get(v_ref, PAD + a + 1, n))
        + get(co, a, n, NORTH) * (v - get(v_ref, PAD + a - 1, n))
    )
    return v, out


def sweep(v_ref, to, co, b_ref, low, high, step):
    for a, n in chunks(low, high):
        v, out = operate(v_ref, co, a, n, step)
        rest = -out if b_ref is None else get(b_ref, a, n) - out
        put(to, PAD + a, v + rest * get(co, a, n, RATE))


def first_sweep(to, co, b_ref, low, high):
    for a, n in chunks(low, high):
        put(to, PAD + a, get(b_ref, a, n) * get(co, a, n, RATE))


def residual(v_ref, to, co, b_ref, low, high, step):
    for a, n in chunks(low, high):
        _, out = operate(v_ref, co, a, n, step)
        put(to, a, -out if b_ref is None else get(b_ref, a, n) - out)


def block_sum(fine, a, n, step, *at):
    return pair_sum(get_strided(fine, 2 * a, n, *at) + get_strided(fine, 2 * a + 1, n, *at), step)


def restrict(fine, to, low, high, step):
    for a, n in chunks(low // 2, high // 2):
        put(to, a, block_sum(fine, a, n, step))


def prolong(coarse, base, to, low, high):
    for a, n in chunks(low // 2, high // 2):
        value = get(coarse, PAD + a, n)
        for p in range(2):
            for h in range(to.shape[0]):
                part = value[:, 128 * h : 128 * h + 128]
                rows = pl.ds(PAD + 2 * a + p, n, stride=2)
                to[h, rows, :] = part if base is None else base[h, rows, :] + part


def diagonal(co, a, n):
    total = get(co, a, n, MASS)
    for k in (EAST, WEST, SOUTH, NORTH):
        total = total + get(co, a, n, k)
    return total


def coarsen(fine, to, rows, step):
    for a, n in chunks(0, rows):
        put(to, a, block_sum(fine, a, n, step, MASS), MASS)
        east = get_strided(fine, 2 * a, n, EAST) + get_strided(fine, 2 * a + 1, n, EAST)
        put(to, a, jnp.where(first_of_pair(east, step), from_east(east, step), east), EAST)
        west = get_strided(fine, 2 * a, n, WEST) + get_strided(fine, 2 * a + 1, n, WEST)
        put(to, a, jnp.where(first_of_pair(west, step), west, from_west(west, step)), WEST)
        put(to, a, pair_sum(get_strided(fine, 2 * a + 1, n, SOUTH), step), SOUTH)
        put(to, a, pair_sum(get_strided(fine, 2 * a, n, NORTH), step), NORTH)


def set_rate(co, rows):
    for a, n in chunks(0, rows):
        d = diagonal(co, a, n)
        put(co, a, RELAX / jnp.where(d > 0, d, 1.0), RATE)


STATE = (208, 112, 64, 96, 48, 192)
STATE_ROWS = sum(STATE)


def state_of(ref):
    starts = [sum(STATE[:k]) for k in range(6)]
    return [ref.at[:, pl.ds(start, count), :] for start, count in zip(starts, STATE)]


def field(*shape):
    return jax.ShapeDtypeStruct(shape, F32)


def scratch(*shape):
    return pltpu.VMEM(shape, F32)


def call(body, outs, scratches, *args, at=pltpu.VMEM, cycles=1000, room=12):
    vmem = pl.BlockSpec(memory_space=pltpu.VMEM)
    return pl.pallas_call(
        body,
        out_shape=outs,
        in_specs=[pl.BlockSpec(memory_space=at)] * len(args),
        out_specs=[vmem] * len(outs) if isinstance(outs, tuple) else vmem,
        scratch_shapes=scratches,
        cost_estimate=pl.CostEstimate(flops=2000 * cycles, bytes_accessed=2000 * cycles, transcendentals=0),
        compiler_params=pltpu.CompilerParams(vmem_limit_bytes=room * 1024 * 1024),
    )(*args)


def prepare(*refs):
    sources, (own, first, second), temps, arrived = refs[:5], refs[5:8], refs[8:13], refs[13]
    copies = [pltpu.make_async_copy(sources[k], temps[k], arrived.at[k]) for k in range(5)]
    for copy in copies:
        copy.start()
    for copy in copies:
        copy.wait()
    right, previous, east, south, mask = temps
    wet = mask[...] > 0
    own[0] = jnp.where(wet, east[...], 0.0)
    own[1] = jnp.where(wet, south[...], 0.0)
    own[2] = jnp.where(wet, right[...], previous[...])
    own[3] = previous[...]
    low = lanes((64, 128)) < 64
    even = lax.rem(lax.axis_index("x"), 2) == 0
    for k in range(2):
        a, b = own[2 * k], pltpu.roll(own[2 * k + 1], 64, 1)
        to_east, to_west = jnp.where(low, b, a), jnp.where(low, a, b)
        first[k] = jnp.where(even, to_east, to_west)
        second[k] = jnp.where(even, to_west, to_east)


def widen(own, second, first, out):
    low = lanes((64, 128)) < 64
    even = lax.rem(lax.axis_index("x"), 2) == 0
    for k in range(2):
        e = jnp.where(even, first[k], second[k])
        w = jnp.where(even, second[k], first[k])
        out[2 * k] = own[2 * k]
        out[2 * k + 1] = own[2 * k + 1]
        out[4 + 2 * k] = jnp.where(low, e, w)
        out[5 + 2 * k] = jnp.where(low, pltpu.roll(e, 64, 1), pltpu.roll(w, 64, 1))


def descend(v1_ref, v2_ref, b1_ref, b2_ref, b3_ref, co, rest, temp, ranges):
    (l0, h0), (l1, h1), (l2, h2), (l3, h3) = ranges
    restrict(rest[0], b1_ref, l0, h0, 1)
    first_sweep(temp[1], co[1], b1_ref, l1, h1)
    sweep(temp[1], v1_ref, co[1], b1_ref, l1, h1, 2)
    residual(v1_ref, rest[1], co[1], b1_ref, l1, h1, 2)
    restrict(rest[1], b2_ref, l1, h1, 2)
    first_sweep(temp[2], co[2], b2_ref, l2, h2)
    sweep(temp[2], v2_ref, co[2], b2_ref, l2, h2, 4)
    residual(v2_ref, rest[2], co[2], b2_ref, l2, h2, 4)
    restrict(rest[2], b3_ref, l3, h3, 4)


def first_leg(own, first, second, co0, co1, co2, state, co3, packed, *temps):
    v0, v1, v2, b1, b2, b0 = state_of(state)
    wet_ref, south_ref, t0, t1, t2, r0, r1, r2, b3 = temps
    even = lax.rem(lax.axis_index("grp"), 2) == 0

    def window(k, a, n):
        part, o = a // 64, a % 64
        if part == 1:
            return jnp.concatenate([own[k, o : o + n, :], own[4 + k, o : o + n, :]], axis=1)
        up, down = (second, first) if part == 0 else (first, second)
        halves = [jnp.where(even, up[h, o : o + n, :], down[h, o : o + n, :]) for h in (k, 4 + k)]
        return jnp.concatenate(halves, axis=1)

    for a, n in chunks(0, 192):
        put(wet_ref, PAD + a, jnp.where(window(0, a, n) > 0, 1.0, 0.0))
        put(v0, PAD + a, window(3, a, n))
        put(b0, a, window(2, a, n))
    for a, n in chunks(0, 192):
        wet = get(wet_ref, PAD + a, n)
        east = window(0, a, n) * from_east(wet, 1)
        south = window(1, a, n) * get(wet_ref, PAD + a + 1, n)
        put(co0, a, east, EAST)
        put(co0, a, from_west(east, 1), WEST)
        put(co0, a, south, SOUTH)
        put(south_ref, PAD + a, south)
        put(co0, a, wet * WET_MASS + (1.0 - wet), MASS)
    for a, n in chunks(0, 192):
        put(co0, a, get(south_ref, PAD + a - 1, n), NORTH)
    set_rate(co0, 192)
    coarsen(co0, co1, 96, 1)
    set_rate(co1, 96)
    coarsen(co1, co2, 48, 2)
    set_rate(co2, 48)
    coarsen(co2, co3, 24, 4)
    set_rate(co3, 24)
    sweep(v0, t0, co0, b0, 0, 192, 1)
    sweep(t0, v0, co0, b0, 0, 192, 1)
    residual(v0, r0, co0, b0, 0, 192, 1)
    descend(
        v1, v2, b1, b2, b3, (co0, co1, co2), (r0, r1, r2), (t0, t1, t2), ((0, 192), (0, 96), (0, 48), (16, 32))
    )
    slot = lanes((8, 128)) & 7
    values = (
        b3[0, 8:16, :],
        co3[MASS, 0, 8:16, :],
        co3[EAST, 0, 8:16, :],
        co3[SOUTH, 0, 8:16, :],
        diagonal(co3, 8, 8)[:, :128],
    )
    out = jnp.zeros((8, 128), F32)
    for k, value in enumerate(values):
        out = jnp.where(slot == k, value, out)
    packed[...] = out


def fan(own, first, second, responded, out):
    even = lax.rem(lax.axis_index("x"), 2) == 0
    east = jnp.where(even, first[...], second[...])
    west = jnp.where(even, second[...], first[...])
    slot = lanes((8, 128)) & 7
    one = jnp.where(slot < 5, own[...], pltpu.roll(west, 5, 1))
    two = jnp.where(slot < 2, pltpu.roll(west, 125, 1), pltpu.roll(east, 2, 1))
    two = jnp.where(slot == 7, responded[...], two)
    for g in range(out.shape[0]):
        out[g, 0] = one
        out[g, 1] = two


def ascend(coarse, bases, sources, to, temp, co):
    ranges = ((32, 160), (8, 88), (0, 48))
    for level in (2, 1, 0):
        low, high = ranges[level]
        step = 1 << level
        prolong(coarse, bases[level], to[level], low, high)
        sweep(to[level], temp[level], co[level], sources[level], low, high, step)
        sweep(temp[level], to[level], co[level], sources[level], low, high, step)
        coarse = to[level]


def second_descent(start, source, kept, rest, temp, co):
    v0, v1, v2, b1, b2, b3 = kept
    sweep(start, temp[0], co[0], source, 32, 160, 1)
    sweep(temp[0], v0, co[0], source, 32, 160, 1)
    residual(v0, rest[0], co[0], source, 32, 160, 1)
    descend(v1, v2, b1, b2, b3, co, rest, temp, ((32, 160), (16, 80), (8, 40), (16, 32)))


def response(co0, co1, co2, co3, state, packed, *temps):
    v0, v1, v2, b1, b2, _ = state_of(state)
    t0, s0, t1, s1, t2, s2, v3, s3, r0, r1, r2, b3 = temps
    put(v3, PAD, jnp.ones((24, 256), F32))
    sweep(v3, s3, co3, None, 0, 24, 8)
    sweep(s3, v3, co3, None, 0, 24, 8)
    none, co = (None, None, None), (co0, co1, co2)
    ascend(v3, none, none, (t0, t1, t2), (s0, s1, s2), co)
    second_descent(t0, None, (v0, v1, v2, b1, b2, b3), (r0, r1, r2), (s0, s1, s2), co)
    packed[...] = b3[0, 8:16, :]


def neighbours():
    group, x = lax.axis_index("grp"), lax.axis_index("x")
    inner_west, inner_east = x > 0, x < 3
    return group, x, inner_west, inner_east, jnp.where(inner_west, x - 1, 3), jnp.where(inner_east, x + 1, 0)


def spread(x, slot):
    at = jnp.bitwise_or(jnp.bitwise_and(lanes(x.shape), 120), slot)
    return jnp.take_along_axis(x, at, axis=1, mode="promise_in_bounds")


def inner_part(wide, to):
    to[0, pl.ds(PAD, 24), :] = wide[1, pl.ds(PAD + 8, 24), :]
    low = lanes((24, 128)) < 64
    to[1, pl.ds(PAD, 24), :] = jnp.where(low, wide[2, pl.ds(PAD + 8, 24), :], wide[0, pl.ds(PAD + 8, 24), :])


def solve_coarse(b3, b4, co3, co4, v3, s3, v4, s4, rest, shift):
    first_sweep(s3, co3, b3, 0, 40)
    sweep(s3, v3, co3, b3, 0, 40, 8)
    residual(v3, rest, co3, b3, 0, 40, 8)
    restrict(rest, b4, 0, 48, 8)
    first_sweep(s4, co4, b4, 0, 24)
    sweep(s4, v4, co4, b4, 0, 24, 16)
    sweep(v4, s4, co4, b4, 0, 24, 16)
    sweep(s4, v4, co4, b4, 0, 24, 16)
    if shift is not None:
        put(v4, PAD, get(v4, PAD, 24) + shift)
    prolong(v4, v3, v3, 0, 40)
    sweep(v3, s3, co3, b3, 8, 32, 8)
    sweep(s3, v3, co3, b3, 8, 32, 8)


def second_leg(gathered, responded, co0, co1, co2, before, co3, co4, after, packed, *temps):
    v0, v1, v2, b1, b2, b0 = state_of(before)
    v0a, v1a, v2a, b1a, b2a, _ = state_of(after)
    (t0, s0, t1, s1, t2, s2, r0, r1, r2, e3, bn, b3, b4, v3, s3, w3, v4, s4, r3, south_ref) = temps
    group = lax.axis_index("grp")
    for t in range(5):
        at = group + (t - 2)
        valid = jnp.logical_and(at >= 0, at < 8).astype(F32)
        at = jnp.clip(at, 0, 7)
        one, two = gathered[at, 0] * valid, gathered[at, 1] * valid

        def wide(k):
            west = spread(one, 5 + k) if k < 3 else spread(two, k - 3)
            return jnp.concatenate([west, spread(one, k), spread(two, 2 + k)], axis=1)

        row = 8 * t
        put(b3, row, wide(0))
        put(co3, row, wide(1), MASS)
        east = wide(2)
        put(co3, row, east, EAST)
        put(co3, row, from_west(east, 8), WEST)
        south = wide(3)
        put(co3, row, south, SOUTH)
        put(south_ref, PAD + row, south)
        d = wide(4)
        put(co3, row, RELAX / jnp.where(d > 0, d, 1.0), RATE)
    for a, n in chunks(0, 40):
        put(co3, a, get(south_ref, PAD + a - 1, n), NORTH)
    coarsen(co3, co4, 20, 8)
    set_rate(co4, 24)

    put(v4, PAD, jnp.ones((24, 384), F32))
    for here, there in ((v4, s4), (s4, v4), (v4, s4), (s4, v4)):
        sweep(here, there, co4, None, 0, 24, 16)
    prolong(v4, None, w3, 0, 40)
    sweep(w3, s3, co3, None, 8, 32, 8)
    sweep(s3, w3, co3, None, 8, 32, 8)
    weight = w3[1, pl.ds(PAD + 16, 8), :]

    solve_coarse(b3, b4, co3, co4, v3, s3, v4, s4, r3, None)
    inner_part(v3, e3)
    co = (co0, co1, co2)
    ascend(e3, (v0, v1, v2), (b0, b1, b2), (t0, t1, t2), (s0, s1, s2), co)
    second_descent(t0, b0, (v0a, v1a, v2a, b1a, b2a, bn), (r0, r1, r2), (s0, s1, s2), co)
    result = bn[0, 8:16, :]
    place = lanes((8, 128))
    slot = place & 7
    out = jnp.where(slot == 0, result, jnp.where(slot == 1, responded[...], 0.0))
    mass = co3[MASS, 1, 16:24, :]
    sums = (mass, weight * b3[1, 16:24, :], weight * result, weight * responded[...])
    for k, value in enumerate(sums):
        once = jnp.where(slot == 0, value, 0.0)
        total = jnp.sum(jnp.sum(once, axis=0, keepdims=True), axis=1, keepdims=True)
        out = jnp.where(place == 8 * k + 6, total, out)
    for z in range(packed.shape[0]):
        packed[z] = out


def relay(gathered, out):
    z = lax.axis_index("z")
    last = gathered.shape[0] - 1
    own = gathered[z]
    before = gathered[jnp.maximum(z - 1, 0)]
    after = gathered[jnp.minimum(z + 1, last)]
    total = gathered[0]
    for k in range(1, last + 1):
        total = total + gathered[k]
    slot = lanes((8, 128)) & 7
    value = jnp.where(slot < 2, own, jnp.where(slot < 4, pltpu.roll(before, 2, 1), pltpu.roll(after, 4, 1)))
    value = jnp.where(slot < 6, value, total)
    for k in range(out.shape[0]):
        out[k] = value


def third_leg(gathered, co0, co1, co2, before, co3, co4, after, beside, *others):
    b0 = state_of(before)[5]
    v0a, v1a, v2a, b1a, b2a, _ = state_of(after)
    v0b, v1b, v2b, b1b, b2b, _ = state_of(beside)
    (surface, rest, *temps) = others
    (t0, s0, c0, t1, s1, c1, d1, t2, s2, c2, d2, e3, b3, b4, v3, s3, v4, s4, r3) = temps
    total = gathered[0]
    for k in range(1, gathered.shape[0]):
        total = total + gathered[k]
    place = lanes((1, 128))
    mass, sum1, sum2a, sum2b = (
        jnp.sum(jnp.where(place == 8 * k + 6, total[:1], 0.0), axis=1, keepdims=True) for k in range(4)
    )
    shift1 = RELAX * sum1 / mass
    shift2 = RELAX * (sum2a + shift1 * sum2b) / mass

    group, x, inner_west, inner_east, at_west, at_east = neighbours()
    for t in range(5):
        g = 4 * jnp.clip(group + (t - 2), 0, 7)
        w, o, e = gathered[g + at_west], gathered[g + x], gathered[g + at_east]
        w = jnp.where(inner_west, w, pltpu.roll(w, 126, 1))
        e = jnp.where(inner_east, e, pltpu.roll(e, 124, 1))
        both = [spread(part + shift1 * from_east(part, 1), 0) for part in (w, o, e)]
        put(b3, 8 * t, jnp.concatenate(both, axis=1))
    solve_coarse(b3, b4, co3, co4, v3, s3, v4, s4, r3, shift2)
    inner_part(v3, e3)

    def combine(to, first, second, offset, low, high):
        for a, n in chunks(offset + low, offset + high):
            put(to, a, get(first, a, n) + shift1 * get(second, a, n))

    combine(c2, v2a, v2b, PAD, 8, 40)
    combine(d2, b2a, b2b, 0, 8, 40)
    combine(c1, v1a, v1b, PAD, 24, 72)
    combine(d1, b1a, b1b, 0, 24, 72)
    combine(c0, v0a, v0b, PAD, 56, 136)
    prolong(e3, c2, t2, 8, 40)
    sweep(t2, s2, co2, d2, 8, 40, 4)
    sweep(s2, t2, co2, d2, 8, 40, 4)
    prolong(t2, c1, t1, 24, 72)
    sweep(t1, s1, co1, d1, 24, 72, 2)
    sweep(s1, t1, co1, d1, 24, 72, 2)
    prolong(t1, c0, t0, 56, 136)
    sweep(t0, s0, co0, b0, 56, 136, 1)
    sweep(s0, t0, co0, b0, 56, 136, 1)
    surface[...] = t0[0, pl.ds(PAD + 64, 64), :]
    for a, n in chunks(64, 128):
        _, out = operate(t0, co0, a, n, 1)
        rest[a - 64 : a - 64 + n, :] = b0[0, a : a + n, :] - out[:, :128]


def swaps(start, count):
    low = range(start, count - 1, 2)
    return [(i, i + 1) for i in low] + [(i + 1, i) for i in low]


def shards(right_side, previous, east_face, south_face, wet_mask):
    dev = ("z", "x")
    own, first, second = call(
        prepare,
        (scratch(4, 64, 128), scratch(2, 64, 128), scratch(2, 64, 128)),
        [*[scratch(64, 128)] * 4, pltpu.VMEM((64, 128), jnp.int32), pltpu.SemaphoreType.DMA((5,))],
        right_side,
        previous,
        east_face,
        south_face,
        wet_mask,
        at=pltpu.HBM,
        room=60,
    )
    first = lax.ppermute(first, dev, swaps(0, 64))
    second = lax.ppermute(second, dev, swaps(1, 64))
    own = call(widen, field(8, 64, 128), [], own, second, first)
    first = lax.ppermute(own, "grp", swaps(0, 8))
    second = lax.ppermute(own, "grp", swaps(1, 8))

    def rows(count, planes=2):
        return field(planes, count, 128)

    def shifted(count, planes=2):
        return field(planes, count + 2 * PAD, 128)

    def as_scratch(*fields):
        return [scratch(*f.shape) for f in fields]

    co = [field(6, 2, count, 128) for count in (192, 96, 48, 24)]
    fine = [shifted(count) for count in (192, 96, 48)]
    sources = [rows(count) for count in (192, 96, 48)]
    state = rows(STATE_ROWS)
    *kept, near, packed = call(
        first_leg,
        (*co[:3], state, co[3], field(8, 128)),
        as_scratch(fine[0], fine[0], *fine, *sources, rows(24)),
        own,
        first,
        second,
    )
    first = lax.ppermute(packed, dev, swaps(0, 64))
    second = lax.ppermute(packed, dev, swaps(1, 64))
    beside, responded = call(
        response,
        (state, field(8, 128)),
        as_scratch(*[f for f in fine for _ in range(2)], shifted(24), shifted(24), *sources, rows(24)),
        *kept[:3],
        near,
        cycles=3000,
    )
    gathered = call(fan, field(8, 2, 8, 128), [], packed, first, second, responded)
    gathered = lax.all_to_all(gathered, "grp", 0, 0, tiled=True)
    coarse = [shifted(40, 3), shifted(40, 3), shifted(40, 3), shifted(24, 3), shifted(24, 3)]
    *second, packed = call(
        second_leg,
        (field(6, 3, 40, 128), field(6, 3, 24, 128), state, field(16, 8, 128)),
        as_scratch(
            *[f for f in fine for _ in range(2)],
            *sources,
            shifted(24),
            rows(24),
            rows(40, 3),
            rows(24, 3),
            *coarse,
            rows(48, 3),
            shifted(40, 3),
        ),
        gathered,
        responded,
        *kept,
    )
    gathered = lax.all_to_all(packed, "z", 0, 0, tiled=True)
    gathered = call(relay, field(32, 8, 128), [], gathered)
    gathered = lax.all_to_all(gathered, ("grp", "x"), 0, 0, tiled=True)
    surface, rest = call(
        third_leg,
        (field(64, 128), field(64, 128)),
        as_scratch(
            *[shifted(192)] * 3,
            *[shifted(96)] * 3,
            rows(96),
            *[shifted(48)] * 3,
            rows(48),
            shifted(24),
            rows(40, 3),
            rows(24, 3),
            shifted(40, 3),
            shifted(40, 3),
            shifted(24, 3),
            shifted(24, 3),
            rows(48, 3),
        ),
        gathered,
        *kept,
        *second,
        beside,
    )
    return surface, rest


def solution(mesh):
    split = Mesh(mesh.devices.reshape(8, 16, 4), ("grp", "z", "x"))
    placed = P("grp", ("z", "x"))
    return jax.shard_map(shards, mesh=split, in_specs=(placed,) * 5, out_specs=(placed,) * 2, check_vma=False)
```

```python
import jax
import jax.numpy as jnp
from jax import lax
from jax.experimental import pallas as pl
from jax.experimental.pallas import tpu as pltpu
from jax.sharding import Mesh
from jax.sharding import PartitionSpec as P

F32 = jnp.float32
RELAX = 0.8
WET_MASS = 2e-05
PAD = 8
CHUNK = 16
EAST, WEST, SOUTH, NORTH, MASS, RATE = range(6)


def lanes(shape):
    return lax.broadcasted_iota(jnp.int32, shape, len(shape) - 1)


def from_east(x, step):
    return pltpu.roll(x, x.shape[1] - step, 1)


def from_west(x, step):
    return pltpu.roll(x, step, 1)


def first_of_pair(x, step):
    return (lanes(x.shape) & step) == 0


def pair_sum(x, step):
    return x + jnp.where(first_of_pair(x, step), from_east(x, step), from_west(x, step))


def get(ref, start, count, *at):
    return jnp.concatenate([ref[(*at, h, pl.ds(start, count), slice(None))] for h in range(ref.shape[len(at)])], axis=1)


def get_strided(ref, start, count, *at):
    return jnp.concatenate(
        [ref[(*at, h, pl.ds(start, count, stride=2), slice(None))] for h in range(ref.shape[len(at)])], axis=1
    )


def put(ref, start, value, *at):
    for h in range(ref.shape[len(at)]):
        ref[(*at, h, pl.ds(start, value.shape[0]), slice(None))] = value[:, 128 * h : 128 * h + 128]


def chunks(low, high, size=CHUNK):
    return [(a, min(size, high - a)) for a in range(low, high, size)]


def operate(v_ref, co, a, n, step):
    v = get(v_ref, PAD + a, n)
    out = (
        get(co, a, n, MASS) * v
        + get(co, a, n, EAST) * (v - from_east(v, step))
        + get(co, a, n, WEST) * (v - from_west(v, step))
        + get(co, a, n, SOUTH) * (v - get(v_ref, PAD + a + 1, n))
        + get(co, a, n, NORTH) * (v - get(v_ref, PAD + a - 1, n))
    )
    return v, out


def sweep(v_ref, to, co, b_ref, low, high, step):
    for a, n in chunks(low, high):
        v, out = operate(v_ref, co, a, n, step)
        rest = -out if b_ref is None else get(b_ref, a, n) - out
        put(to, PAD + a, v + rest * get(co, a, n, RATE))


def first_sweep(to, co, b_ref, low, high):
    for a, n in chunks(low, high):
        put(to, PAD + a, get(b_ref, a, n) * get(co, a, n, RATE))


def residual(v_ref, to, co, b_ref, low, high, step):
    for a, n in chunks(low, high):
        _, out = operate(v_ref, co, a, n, step)
        put(to, a, -out if b_ref is None else get(b_ref, a, n) - out)


def block_sum(fine, a, n, step, *at):
    return pair_sum(get_strided(fine, 2 * a, n, *at) + get_strided(fine, 2 * a + 1, n, *at), step)


def restrict(fine, to, low, high, step):
    for a, n in chunks(low // 2, high // 2):
        put(to, a, block_sum(fine, a, n, step))


def prolong(coarse, base, to, low, high):
    for a, n in chunks(low // 2, high // 2):
        value = get(coarse, PAD + a, n)
        for p in range(2):
            for h in range(to.shape[0]):
                part = value[:, 128 * h : 128 * h + 128]
                rows = pl.ds(PAD + 2 * a + p, n, stride=2)
                to[h, rows, :] = part if base is None else base[h, rows, :] + part


def diagonal(co, a, n):
    total = get(co, a, n, MASS)
    for k in (EAST, WEST, SOUTH, NORTH):
        total = total + get(co, a, n, k)
    return total


def coarsen(fine, to, rows, step):
    for a, n in chunks(0, rows):
        put(to, a, block_sum(fine, a, n, step, MASS), MASS)
        east = get_strided(fine, 2 * a, n, EAST) + get_strided(fine, 2 * a + 1, n, EAST)
        put(to, a, jnp.where(first_of_pair(east, step), from_east(east, step), east), EAST)
        west = get_strided(fine, 2 * a, n, WEST) + get_strided(fine, 2 * a + 1, n, WEST)
        put(to, a, jnp.where(first_of_pair(west, step), west, from_west(west, step)), WEST)
        put(to, a, pair_sum(get_strided(fine, 2 * a + 1, n, SOUTH), step), SOUTH)
        put(to, a, pair_sum(get_strided(fine, 2 * a, n, NORTH), step), NORTH)


def set_rate(co, rows):
    for a, n in chunks(0, rows):
        d = diagonal(co, a, n)
        put(co, a, RELAX / jnp.where(d > 0, d, 1.0), RATE)


STATE = (208, 112, 64, 96, 48, 192)
STATE_ROWS = sum(STATE)


def state_of(ref):
    starts = [sum(STATE[:k]) for k in range(6)]
    return [ref.at[:, pl.ds(start, count), :] for start, count in zip(starts, STATE)]


def field(*shape):
    return jax.ShapeDtypeStruct(shape, F32)


def scratch(*shape):
    return pltpu.VMEM(shape, F32)


def call(body, outs, scratches, *args, at=pltpu.VMEM, cycles=1000, room=12):
    vmem = pl.BlockSpec(memory_space=pltpu.VMEM)
    return pl.pallas_call(
        body,
        out_shape=outs,
        in_specs=[pl.BlockSpec(memory_space=at)] * len(args),
        out_specs=[vmem] * len(outs) if isinstance(outs, tuple) else vmem,
        scratch_shapes=scratches,
        cost_estimate=pl.CostEstimate(flops=2000 * cycles, bytes_accessed=2000 * cycles, transcendentals=0),
        compiler_params=pltpu.CompilerParams(vmem_limit_bytes=room * 1024 * 1024),
    )(*args)


def prepare(*refs):
    sources, (own, first, second), temps, arrived = refs[:5], refs[5:8], refs[8:13], refs[13]
    copies = [pltpu.make_async_copy(sources[k], temps[k], arrived.at[k]) for k in range(5)]
    for copy in copies:
        copy.start()
    for copy in copies:
        copy.wait()
    right, previous, east, south, mask = temps
    wet = mask[...] > 0
    own[0] = jnp.where(wet, east[...], 0.0)
    own[1] = jnp.where(wet, south[...], 0.0)
    own[2] = jnp.where(wet, right[...], previous[...])
    own[3] = previous[...]
    low = lanes((64, 128)) < 64
    even = lax.rem(lax.axis_index("x"), 2) == 0
    for k in range(2):
        a, b = own[2 * k], pltpu.roll(own[2 * k + 1], 64, 1)
        to_east, to_west = jnp.where(low, b, a), jnp.where(low, a, b)
        first[k] = jnp.where(even, to_east, to_west)
        second[k] = jnp.where(even, to_west, to_east)


def widen(own, second, first, out, near, far, wet_ref, before_ref, south_ref):
    low = lanes((64, 128)) < 64
    even = lax.rem(lax.axis_index("x"), 2) == 0
    for k in range(2):
        e = jnp.where(even, first[k], second[k])
        w = jnp.where(even, second[k], first[k])
        for p, (east, west) in enumerate(((e, w), (pltpu.roll(e, 64, 1), pltpu.roll(w, 64, 1)))):
            out[0, pl.ds(64 * (2 * k + p), 64), :] = own[2 * k + p]
            out[1, pl.ds(64 * (2 * k + p), 64), :] = jnp.where(low, east, west)
    for ref in (wet_ref, before_ref, south_ref):
        for edge in (0, PAD + 64):
            put(ref, edge, jnp.zeros((PAD, 256), F32))
    for a, n in chunks(0, 64):
        put(wet_ref, PAD + a, jnp.where(get(out, a, n) > 0, 1.0, 0.0))
        put(before_ref, PAD + a, get(out, 192 + a, n))
    for a, n in chunks(0, 64):
        put(south_ref, PAD + a, get(out, 64 + a, n) * get(wet_ref, PAD + a + 1, n))
    for a, n in chunks(0, 64):
        wet, v = get(wet_ref, PAD + a, n), get(before_ref, PAD + a, n)
        east = get(out, a, n) * from_east(wet, 1)
        applied = (
            (wet * WET_MASS + (1.0 - wet)) * v
            + east * (v - from_east(v, 1))
            + from_west(east, 1) * (v - from_west(v, 1))
            + get(south_ref, PAD + a, n) * (v - get(before_ref, PAD + a + 1, n))
            + get(south_ref, PAD + a - 1, n) * (v - get(before_ref, PAD + a - 1, n))
        )
        put(out, 128 + a, get(out, 128 + a, n) - applied)
    group_even = lax.rem(lax.axis_index("grp"), 2) == 0
    for k in range(4):
        count = 56 if k < 3 else 8
        for h in range(2):
            up, down = out[h, pl.ds(64 * k, count), :], out[h, pl.ds(64 * k + 64 - count, count), :]
            near[h, pl.ds(56 * k, count), :] = jnp.where(group_even, down, up)
            far[h, pl.ds(56 * k, count), :] = jnp.where(group_even, up, down)


def descend(v1_ref, v2_ref, b1_ref, b2_ref, b3_ref, co, rest, temp, ranges):
    (l0, h0), (l1, h1), (l2, h2), (l3, h3) = ranges
    restrict(rest[0], b1_ref, l0, h0, 1)
    first_sweep(temp[1], co[1], b1_ref, l1, h1)
    sweep(temp[1], v1_ref, co[1], b1_ref, l1, h1, 2)
    residual(v1_ref, rest[1], co[1], b1_ref, l1, h1, 2)
    restrict(rest[1], b2_ref, l1, h1, 2)
    first_sweep(temp[2], co[2], b2_ref, l2, h2)
    sweep(temp[2], v2_ref, co[2], b2_ref, l2, h2, 4)
    residual(v2_ref, rest[2], co[2], b2_ref, l2, h2, 4)
    restrict(rest[2], b3_ref, l3, h3, 4)


def first_leg(own, far, near, co0, co1, co2, state, co3, packed, *temps):
    v0, v1, v2, b1, b2, b0 = state_of(state)
    wet_ref, south_ref, t0, t1, t2, r0, r1, r2, b3 = temps
    even = lax.rem(lax.axis_index("grp"), 2) == 0

    def above(start, n):
        return jnp.where(even, get(far, start, n), get(near, start, n))

    def below(start, n):
        return jnp.where(even, get(near, start, n), get(far, start, n))

    def window(k, a, n):
        if a < 8 or a >= 184:
            return jnp.zeros((n, 256), F32)
        if a < 64:
            return above(56 * k + a - 8, n)
        return get(own, 64 * k + a - 64, n) if a < 128 else below(56 * k + a - 128, n)

    for a, n in chunks(0, 192, 8):
        put(wet_ref, PAD + a, jnp.where(window(0, a, n) > 0, 1.0, 0.0))
        put(b0, a, window(2, a, n))
    for a, n in chunks(0, 192, 8):
        wet = get(wet_ref, PAD + a, n)
        east = window(0, a, n) * from_east(wet, 1)
        south = window(1, a, n) * get(wet_ref, PAD + a + 1, n)
        put(co0, a, east, EAST)
        put(co0, a, from_west(east, 1), WEST)
        put(co0, a, south, SOUTH)
        put(south_ref, PAD + a, south)
        put(co0, a, wet * WET_MASS + (1.0 - wet), MASS)
    edges = ((63, above(175, 1), get(own, 192, 1)), (127, get(own, 255, 1), below(168, 1)))
    for row, here, next_row in edges:
        flow = get(co0, row, 1, SOUTH) * (here - next_row)
        put(b0, row, get(b0, row, 1) - flow)
        put(b0, row + 1, get(b0, row + 1, 1) + flow)
    for a, n in chunks(0, 192):
        put(co0, a, get(south_ref, PAD + a - 1, n), NORTH)
    set_rate(co0, 192)
    coarsen(co0, co1, 96, 1)
    set_rate(co1, 96)
    coarsen(co1, co2, 48, 2)
    set_rate(co2, 48)
    coarsen(co2, co3, 24, 4)
    set_rate(co3, 24)
    first_sweep(t0, co0, b0, 0, 192)
    sweep(t0, v0, co0, b0, 0, 192, 1)
    residual(v0, r0, co0, b0, 0, 192, 1)
    descend(
        v1, v2, b1, b2, b3, (co0, co1, co2), (r0, r1, r2), (t0, t1, t2), ((0, 192), (0, 96), (0, 48), (16, 32))
    )
    slot = lanes((8, 128)) & 7
    values = (
        b3[0, 8:16, :],
        co3[MASS, 0, 8:16, :],
        co3[EAST, 0, 8:16, :],
        co3[SOUTH, 0, 8:16, :],
        diagonal(co3, 8, 8)[:, :128],
    )
    out = jnp.zeros((8, 128), F32)
    for k, value in enumerate(values):
        out = jnp.where(slot == k, value, out)
    packed[...] = out


def fan(own, first, second, responded, out):
    even = lax.rem(lax.axis_index("x"), 2) == 0
    east = jnp.where(even, first[...], second[...])
    west = jnp.where(even, second[...], first[...])
    slot = lanes((8, 128)) & 7
    one = jnp.where(slot < 5, own[...], pltpu.roll(west, 5, 1))
    two = jnp.where(slot < 2, pltpu.roll(west, 125, 1), pltpu.roll(east, 2, 1))
    two = jnp.where(slot == 7, responded[...], two)
    for g in range(out.shape[0]):
        out[g, 0] = one
        out[g, 1] = two


def ascend(coarse, bases, sources, to, temp, co):
    ranges = ((32, 160), (8, 88), (0, 48))
    for level in (2, 1, 0):
        low, high = ranges[level]
        step = 1 << level
        prolong(coarse, bases[level], to[level], low, high)
        sweep(to[level], temp[level], co[level], sources[level], low, high, step)
        sweep(temp[level], to[level], co[level], sources[level], low, high, step)
        coarse = to[level]


def second_descent(start, source, kept, rest, temp, co):
    v0, v1, v2, b1, b2, b3 = kept
    sweep(start, temp[0], co[0], source, 32, 160, 1)
    sweep(temp[0], v0, co[0], source, 32, 160, 1)
    residual(v0, rest[0], co[0], source, 32, 160, 1)
    descend(v1, v2, b1, b2, b3, co, rest, temp, ((32, 160), (16, 80), (8, 40), (16, 32)))


def response(co0, co1, co2, co3, state, packed, *temps):
    v0, v1, v2, b1, b2, _ = state_of(state)
    t0, s0, t1, s1, t2, s2, v3, s3, r0, r1, r2, b3 = temps
    put(v3, PAD, jnp.ones((24, 256), F32))
    sweep(v3, s3, co3, None, 0, 24, 8)
    sweep(s3, v3, co3, None, 0, 24, 8)
    none, co = (None, None, None), (co0, co1, co2)
    ascend(v3, none, none, (t0, t1, t2), (s0, s1, s2), co)
    second_descent(t0, None, (v0, v1, v2, b1, b2, b3), (r0, r1, r2), (s0, s1, s2), co)
    packed[...] = b3[0, 8:16, :]


def neighbours():
    group, x = lax.axis_index("grp"), lax.axis_index("x")
    inner_west, inner_east = x > 0, x < 3
    return group, x, inner_west, inner_east, jnp.where(inner_west, x - 1, 3), jnp.where(inner_east, x + 1, 0)


def spread(x, slot):
    at = jnp.bitwise_or(jnp.bitwise_and(lanes(x.shape), 120), slot)
    return jnp.take_along_axis(x, at, axis=1, mode="promise_in_bounds")


def inner_part(wide, to):
    to[0, pl.ds(PAD, 24), :] = wide[1, pl.ds(PAD + 8, 24), :]
    low = lanes((24, 128)) < 64
    to[1, pl.ds(PAD, 24), :] = jnp.where(low, wide[2, pl.ds(PAD + 8, 24), :], wide[0, pl.ds(PAD + 8, 24), :])


def solve_coarse(b3, b4, co3, co4, v3, s3, v4, s4, rest, shift):
    first_sweep(s3, co3, b3, 0, 40)
    sweep(s3, v3, co3, b3, 0, 40, 8)
    residual(v3, rest, co3, b3, 0, 40, 8)
    restrict(rest, b4, 0, 48, 8)
    first_sweep(s4, co4, b4, 0, 24)
    sweep(s4, v4, co4, b4, 0, 24, 16)
    sweep(v4, s4, co4, b4, 0, 24, 16)
    sweep(s4, v4, co4, b4, 0, 24, 16)
    if shift is not None:
        put(v4, PAD, get(v4, PAD, 24) + shift)
    prolong(v4, v3, v3, 0, 40)
    sweep(v3, s3, co3, b3, 8, 32, 8)
    sweep(s3, v3, co3, b3, 8, 32, 8)


def second_leg(gathered, responded, co0, co1, co2, before, co3, co4, after, packed, *temps):
    v0, v1, v2, b1, b2, b0 = state_of(before)
    v0a, v1a, v2a, b1a, b2a, _ = state_of(after)
    (t0, s0, t1, s1, t2, s2, r0, r1, r2, e3, bn, b3, b4, v3, s3, w3, v4, s4, r3, south_ref) = temps
    group = lax.axis_index("grp")
    for t in range(5):
        at = group + (t - 2)
        valid = jnp.logical_and(at >= 0, at < 8).astype(F32)
        at = jnp.clip(at, 0, 7)
        one, two = gathered[at, 0] * valid, gathered[at, 1] * valid

        def wide(k):
            west = spread(one, 5 + k) if k < 3 else spread(two, k - 3)
            return jnp.concatenate([west, spread(one, k), spread(two, 2 + k)], axis=1)

        row = 8 * t
        put(b3, row, wide(0))
        put(co3, row, wide(1), MASS)
        east = wide(2)
        put(co3, row, east, EAST)
        put(co3, row, from_west(east, 8), WEST)
        south = wide(3)
        put(co3, row, south, SOUTH)
        put(south_ref, PAD + row, south)
        d = wide(4)
        put(co3, row, RELAX / jnp.where(d > 0, d, 1.0), RATE)
    for a, n in chunks(0, 40):
        put(co3, a, get(south_ref, PAD + a - 1, n), NORTH)
    coarsen(co3, co4, 20, 8)
    set_rate(co4, 24)

    put(v4, PAD, jnp.ones((24, 384), F32))
    for here, there in ((v4, s4), (s4, v4), (v4, s4), (s4, v4)):
        sweep(here, there, co4, None, 0, 24, 16)
    prolong(v4, None, w3, 0, 40)
    sweep(w3, s3, co3, None, 8, 32, 8)
    sweep(s3, w3, co3, None, 8, 32, 8)
    weight = w3[1, pl.ds(PAD + 16, 8), :]

    solve_coarse(b3, b4, co3, co4, v3, s3, v4, s4, r3, None)
    inner_part(v3, e3)
    co = (co0, co1, co2)
    ascend(e3, (v0, v1, v2), (b0, b1, b2), (t0, t1, t2), (s0, s1, s2), co)
    second_descent(t0, b0, (v0a, v1a, v2a, b1a, b2a, bn), (r0, r1, r2), (s0, s1, s2), co)
    result = bn[0, 8:16, :]
    place = lanes((8, 128))
    slot = place & 7
    out = jnp.where(slot == 0, result, jnp.where(slot == 1, responded[...], 0.0))
    mass = co3[MASS, 1, 16:24, :]
    sums = (mass, weight * b3[1, 16:24, :], weight * result, weight * responded[...])
    for k, value in enumerate(sums):
        once = jnp.where(slot == 0, value, 0.0)
        total = jnp.sum(jnp.sum(once, axis=0, keepdims=True), axis=1, keepdims=True)
        out = jnp.where(place == 8 * k + 6, total, out)
    for z in range(packed.shape[0]):
        packed[z] = out


def relay(gathered, out):
    z = lax.axis_index("z")
    last = gathered.shape[0] - 1
    own = gathered[z]
    before = gathered[jnp.maximum(z - 1, 0)]
    after = gathered[jnp.minimum(z + 1, last)]
    total = gathered[0]
    for k in range(1, last + 1):
        total = total + gathered[k]
    slot = lanes((8, 128)) & 7
    value = jnp.where(slot < 2, own, jnp.where(slot < 4, pltpu.roll(before, 2, 1), pltpu.roll(after, 4, 1)))
    value = jnp.where(slot < 6, value, total)
    for k in range(out.shape[0]):
        out[k] = value


def third_leg(gathered, own, co0, co1, co2, before, co3, co4, after, beside, *others):
    b0 = state_of(before)[5]
    v0a, v1a, v2a, b1a, b2a, _ = state_of(after)
    v0b, v1b, v2b, b1b, b2b, _ = state_of(beside)
    (surface, rest, *temps) = others
    (t0, s0, c0, t1, s1, c1, d1, t2, s2, c2, d2, e3, b3, b4, v3, s3, v4, s4, r3) = temps
    total = gathered[0]
    for k in range(1, gathered.shape[0]):
        total = total + gathered[k]
    place = lanes((1, 128))
    mass, sum1, sum2a, sum2b = (
        jnp.sum(jnp.where(place == 8 * k + 6, total[:1], 0.0), axis=1, keepdims=True) for k in range(4)
    )
    shift1 = RELAX * sum1 / mass
    shift2 = RELAX * (sum2a + shift1 * sum2b) / mass

    group, x, inner_west, inner_east, at_west, at_east = neighbours()
    for t in range(5):
        g = 4 * jnp.clip(group + (t - 2), 0, 7)
        w, o, e = gathered[g + at_west], gathered[g + x], gathered[g + at_east]
        w = jnp.where(inner_west, w, pltpu.roll(w, 126, 1))
        e = jnp.where(inner_east, e, pltpu.roll(e, 124, 1))
        both = [spread(part + shift1 * from_east(part, 1), 0) for part in (w, o, e)]
        put(b3, 8 * t, jnp.concatenate(both, axis=1))
    solve_coarse(b3, b4, co3, co4, v3, s3, v4, s4, r3, shift2)
    inner_part(v3, e3)

    def combine(to, first, second, offset, low, high):
        for a, n in chunks(offset + low, offset + high):
            put(to, a, get(first, a, n) + shift1 * get(second, a, n))

    combine(c2, v2a, v2b, PAD, 8, 40)
    combine(d2, b2a, b2b, 0, 8, 40)
    combine(c1, v1a, v1b, PAD, 24, 72)
    combine(d1, b1a, b1b, 0, 24, 72)
    combine(c0, v0a, v0b, PAD, 56, 136)
    prolong(e3, c2, t2, 8, 40)
    sweep(t2, s2, co2, d2, 8, 40, 4)
    sweep(s2, t2, co2, d2, 8, 40, 4)
    prolong(t2, c1, t1, 24, 72)
    sweep(t1, s1, co1, d1, 24, 72, 2)
    sweep(s1, t1, co1, d1, 24, 72, 2)
    prolong(t1, c0, t0, 56, 136)
    sweep(t0, s0, co0, b0, 56, 136, 1)
    sweep(s0, t0, co0, b0, 56, 136, 1)
    surface[...] = own[0, pl.ds(192, 64), :] + t0[0, pl.ds(PAD + 64, 64), :]
    for a, n in chunks(64, 128):
        _, out = operate(t0, co0, a, n, 1)
        rest[a - 64 : a - 64 + n, :] = b0[0, a : a + n, :] - out[:, :128]


def swaps(start, count):
    low = range(start, count - 1, 2)
    return [(i, i + 1) for i in low] + [(i + 1, i) for i in low]


def shards(right_side, previous, east_face, south_face, wet_mask):
    dev = ("z", "x")
    own, first, second = call(
        prepare,
        (scratch(4, 64, 128), scratch(2, 64, 128), scratch(2, 64, 128)),
        [*[scratch(64, 128)] * 4, pltpu.VMEM((64, 128), jnp.int32), pltpu.SemaphoreType.DMA((5,))],
        right_side,
        previous,
        east_face,
        south_face,
        wet_mask,
        at=pltpu.HBM,
        room=60,
    )
    first = lax.ppermute(first, dev, swaps(0, 64))
    second = lax.ppermute(second, dev, swaps(1, 64))
    own, near, far = call(
        widen,
        (field(2, 256, 128), field(2, 176, 128), field(2, 176, 128)),
        [scratch(2, 80, 128)] * 3,
        own,
        second,
        first,
    )
    far = lax.ppermute(far, "grp", swaps(1, 8))
    near = lax.ppermute(near, "grp", swaps(0, 8))

    def rows(count, planes=2):
        return field(planes, count, 128)

    def shifted(count, planes=2):
        return field(planes, count + 2 * PAD, 128)

    def as_scratch(*fields):
        return [scratch(*f.shape) for f in fields]

    co = [field(6, 2, count, 128) for count in (192, 96, 48, 24)]
    fine = [shifted(count) for count in (192, 96, 48)]
    sources = [rows(count) for count in (192, 96, 48)]
    state = rows(STATE_ROWS)
    *kept, near, packed = call(
        first_leg,
        (*co[:3], state, co[3], field(8, 128)),
        as_scratch(fine[0], fine[0], *fine, *sources, rows(24)),
        own,
        far,
        near,
    )
    first = lax.ppermute(packed, dev, swaps(0, 64))
    second = lax.ppermute(packed, dev, swaps(1, 64))
    beside, responded = call(
        response,
        (state, field(8, 128)),
        as_scratch(*[f for f in fine for _ in range(2)], shifted(24), shifted(24), *sources, rows(24)),
        *kept[:3],
        near,
        cycles=3000,
    )
    gathered = call(fan, field(8, 2, 8, 128), [], packed, first, second, responded)
    gathered = lax.all_to_all(gathered, "grp", 0, 0, tiled=True)
    coarse = [shifted(40, 3), shifted(40, 3), shifted(40, 3), shifted(24, 3), shifted(24, 3)]
    *second, packed = call(
        second_leg,
        (field(6, 3, 40, 128), field(6, 3, 24, 128), state, field(16, 8, 128)),
        as_scratch(
            *[f for f in fine for _ in range(2)],
            *sources,
            shifted(24),
            rows(24),
            rows(40, 3),
            rows(24, 3),
            *coarse,
            rows(48, 3),
            shifted(40, 3),
        ),
        gathered,
        responded,
        *kept,
    )
    gathered = lax.all_to_all(packed, "z", 0, 0, tiled=True)
    gathered = call(relay, field(32, 8, 128), [], gathered)
    gathered = lax.all_to_all(gathered, ("grp", "x"), 0, 0, tiled=True)
    surface, rest = call(
        third_leg,
        (field(64, 128), field(64, 128)),
        as_scratch(
            *[shifted(192)] * 3,
            *[shifted(96)] * 3,
            rows(96),
            *[shifted(48)] * 3,
            rows(48),
            shifted(24),
            rows(40, 3),
            rows(24, 3),
            shifted(40, 3),
            shifted(40, 3),
            shifted(24, 3),
            shifted(24, 3),
            rows(48, 3),
        ),
        gathered,
        own,
        *kept,
        *second,
        beside,
    )
    return surface, rest


def solution(mesh):
    split = Mesh(mesh.devices.reshape(8, 16, 4), ("grp", "z", "x"))
    placed = P("grp", ("z", "x"))
    return jax.shard_map(shards, mesh=split, in_specs=(placed,) * 5, out_specs=(placed,) * 2, check_vma=False)
```

```python
import jax
import jax.numpy as jnp
from jax import lax
from jax.experimental import pallas as pl
from jax.experimental.pallas import tpu as pltpu
from jax.sharding import Mesh
from jax.sharding import PartitionSpec as P

F32 = jnp.float32
RELAX = 0.8
WET_MASS = 2e-05
PAD = 8
CHUNK = 8
EAST, WEST, SOUTH, NORTH, MASS, RATE = range(6)


def lanes(shape):
    return lax.broadcasted_iota(jnp.int32, shape, len(shape) - 1)


def from_east(x, step):
    return pltpu.roll(x, x.shape[1] - step, 1)


def from_west(x, step):
    return pltpu.roll(x, step, 1)


def first_of_pair(x, step):
    return (lanes(x.shape) & step) == 0


def pair_sum(x, step):
    return x + jnp.where(first_of_pair(x, step), from_east(x, step), from_west(x, step))


def get(ref, start, count, *at):
    return jnp.concatenate([ref[(*at, h, pl.ds(start, count), slice(None))] for h in range(ref.shape[len(at)])], axis=1)


def get_strided(ref, start, count, *at):
    return jnp.concatenate(
        [ref[(*at, h, pl.ds(start, count, stride=2), slice(None))] for h in range(ref.shape[len(at)])], axis=1
    )


def put(ref, start, value, *at):
    for h in range(ref.shape[len(at)]):
        ref[(*at, h, pl.ds(start, value.shape[0]), slice(None))] = value[:, 128 * h : 128 * h + 128]


def chunks(low, high, size=CHUNK):
    return [(a, min(size, high - a)) for a in range(low, high, size)]


def operate(v_ref, co, a, n, step):
    v = get(v_ref, PAD + a, n)
    out = (
        get(co, a, n, MASS) * v
        + get(co, a, n, EAST) * (v - from_east(v, step))
        + get(co, a, n, WEST) * (v - from_west(v, step))
        + get(co, a, n, SOUTH) * (v - get(v_ref, PAD + a + 1, n))
        + get(co, a, n, NORTH) * (v - get(v_ref, PAD + a - 1, n))
    )
    return v, out


def sweep(v_ref, to, co, b_ref, low, high, step):
    for a, n in chunks(low, high):
        v, out = operate(v_ref, co, a, n, step)
        rest = -out if b_ref is None else get(b_ref, a, n) - out
        put(to, PAD + a, v + rest * get(co, a, n, RATE))


def first_sweep(to, co, b_ref, low, high):
    for a, n in chunks(low, high):
        put(to, PAD + a, get(b_ref, a, n) * get(co, a, n, RATE))


def residual(v_ref, to, co, b_ref, low, high, step):
    for a, n in chunks(low, high):
        _, out = operate(v_ref, co, a, n, step)
        put(to, a, -out if b_ref is None else get(b_ref, a, n) - out)


def block_sum(fine, a, n, step, *at):
    return pair_sum(get_strided(fine, 2 * a, n, *at) + get_strided(fine, 2 * a + 1, n, *at), step)


def restrict(fine, to, low, high, step):
    for a, n in chunks(low // 2, high // 2):
        put(to, a, block_sum(fine, a, n, step))


def prolong(coarse, base, to, low, high):
    for a, n in chunks(low // 2, high // 2):
        value = get(coarse, PAD + a, n)
        for p in range(2):
            for h in range(to.shape[0]):
                part = value[:, 128 * h : 128 * h + 128]
                rows = pl.ds(PAD + 2 * a + p, n, stride=2)
                to[h, rows, :] = part if base is None else base[h, rows, :] + part


def diagonal(co, a, n):
    total = get(co, a, n, MASS)
    for k in (EAST, WEST, SOUTH, NORTH):
        total = total + get(co, a, n, k)
    return total


def coarsen(fine, to, rows, step):
    for a, n in chunks(0, rows):
        put(to, a, block_sum(fine, a, n, step, MASS), MASS)
        east = get_strided(fine, 2 * a, n, EAST) + get_strided(fine, 2 * a + 1, n, EAST)
        put(to, a, jnp.where(first_of_pair(east, step), from_east(east, step), east), EAST)
        west = get_strided(fine, 2 * a, n, WEST) + get_strided(fine, 2 * a + 1, n, WEST)
        put(to, a, jnp.where(first_of_pair(west, step), west, from_west(west, step)), WEST)
        put(to, a, pair_sum(get_strided(fine, 2 * a + 1, n, SOUTH), step), SOUTH)
        put(to, a, pair_sum(get_strided(fine, 2 * a, n, NORTH), step), NORTH)


def set_rate(co, rows):
    for a, n in chunks(0, rows):
        d = diagonal(co, a, n)
        put(co, a, RELAX / jnp.where(d > 0, d, 1.0), RATE)


STATE = (208, 112, 64, 96, 48, 192)
STATE_ROWS = sum(STATE)


def state_of(ref):
    starts = [sum(STATE[:k]) for k in range(6)]
    return [ref.at[:, pl.ds(start, count), :] for start, count in zip(starts, STATE)]


def field(*shape):
    return jax.ShapeDtypeStruct(shape, F32)


def scratch(*shape):
    return pltpu.VMEM(shape, F32)


def call(body, outs, scratches, *args, at=pltpu.VMEM, cycles=1000, room=12):
    vmem = pl.BlockSpec(memory_space=pltpu.VMEM)
    return pl.pallas_call(
        body,
        out_shape=outs,
        in_specs=[pl.BlockSpec(memory_space=at)] * len(args),
        out_specs=[vmem] * len(outs) if isinstance(outs, tuple) else vmem,
        scratch_shapes=scratches,
        cost_estimate=pl.CostEstimate(flops=2000 * cycles, bytes_accessed=2000 * cycles, transcendentals=0),
        compiler_params=pltpu.CompilerParams(vmem_limit_bytes=room * 1024 * 1024),
    )(*args)


def prepare(*refs):
    sources, (own, first, second), temps, arrived = refs[:5], refs[5:8], refs[8:13], refs[13]
    copies = [pltpu.make_async_copy(sources[k], temps[k], arrived.at[k]) for k in range(5)]
    for copy in copies:
        copy.start()
    for copy in copies:
        copy.wait()
    right, previous, east, south, mask = temps
    wet = mask[...] > 0
    own[0] = jnp.where(wet, east[...], 0.0)
    own[1] = jnp.where(wet, south[...], 0.0)
    own[2] = jnp.where(wet, right[...], previous[...])
    own[3] = previous[...]
    low = lanes((64, 128)) < 64
    even = lax.rem(lax.axis_index("x"), 2) == 0
    for k in range(2):
        a, b = own[2 * k], pltpu.roll(own[2 * k + 1], 64, 1)
        to_east, to_west = jnp.where(low, b, a), jnp.where(low, a, b)
        first[k] = jnp.where(even, to_east, to_west)
        second[k] = jnp.where(even, to_west, to_east)


def widen(own, second, first, out, near, far, wet_ref, before_ref, south_ref):
    low = lanes((64, 128)) < 64
    even = lax.rem(lax.axis_index("x"), 2) == 0
    for k in range(2):
        e = jnp.where(even, first[k], second[k])
        w = jnp.where(even, second[k], first[k])
        for p, (east, west) in enumerate(((e, w), (pltpu.roll(e, 64, 1), pltpu.roll(w, 64, 1)))):
            out[0, pl.ds(64 * (2 * k + p), 64), :] = own[2 * k + p]
            out[1, pl.ds(64 * (2 * k + p), 64), :] = jnp.where(low, east, west)
    for ref in (wet_ref, before_ref, south_ref):
        for edge in (0, PAD + 64):
            put(ref, edge, jnp.zeros((PAD, 256), F32))
    for a, n in chunks(0, 64):
        put(wet_ref, PAD + a, jnp.where(get(out, a, n) > 0, 1.0, 0.0))
        put(before_ref, PAD + a, get(out, 192 + a, n))
    for a, n in chunks(0, 64):
        put(south_ref, PAD + a, get(out, 64 + a, n) * get(wet_ref, PAD + a + 1, n))
    for a, n in chunks(0, 64):
        wet, v = get(wet_ref, PAD + a, n), get(before_ref, PAD + a, n)
        east = get(out, a, n) * from_east(wet, 1)
        applied = (
            (wet * WET_MASS + (1.0 - wet)) * v
            + east * (v - from_east(v, 1))
            + from_west(east, 1) * (v - from_west(v, 1))
            + get(south_ref, PAD + a, n) * (v - get(before_ref, PAD + a + 1, n))
            + get(south_ref, PAD + a - 1, n) * (v - get(before_ref, PAD + a - 1, n))
        )
        put(out, 128 + a, get(out, 128 + a, n) - applied)
    group_even = lax.rem(lax.axis_index("grp"), 2) == 0
    for k in range(4):
        count = 56 if k < 3 else 8
        for h in range(2):
            up, down = out[h, pl.ds(64 * k, count), :], out[h, pl.ds(64 * k + 64 - count, count), :]
            near[h, pl.ds(56 * k, count), :] = jnp.where(group_even, down, up)
            far[h, pl.ds(56 * k, count), :] = jnp.where(group_even, up, down)


def descend(v1_ref, v2_ref, b1_ref, b2_ref, b3_ref, co, rest, temp, ranges):
    (l0, h0), (l1, h1), (l2, h2), (l3, h3) = ranges
    restrict(rest[0], b1_ref, l0, h0, 1)
    first_sweep(temp[1], co[1], b1_ref, l1, h1)
    sweep(temp[1], v1_ref, co[1], b1_ref, l1, h1, 2)
    residual(v1_ref, rest[1], co[1], b1_ref, l1, h1, 2)
    restrict(rest[1], b2_ref, l1, h1, 2)
    first_sweep(temp[2], co[2], b2_ref, l2, h2)
    sweep(temp[2], v2_ref, co[2], b2_ref, l2, h2, 4)
    residual(v2_ref, rest[2], co[2], b2_ref, l2, h2, 4)
    restrict(rest[2], b3_ref, l3, h3, 4)


def first_leg(own, far, near, co0, co1, co2, state, co3, packed, *temps):
    v0, v1, v2, b1, b2, b0 = state_of(state)
    wet_ref, south_ref, t0, t1, t2, r0, r1, r2, b3 = temps
    even = lax.rem(lax.axis_index("grp"), 2) == 0

    def above(start, n):
        return jnp.where(even, get(far, start, n), get(near, start, n))

    def below(start, n):
        return jnp.where(even, get(near, start, n), get(far, start, n))

    def window(k, a, n):
        if a < 8 or a >= 184:
            return jnp.zeros((n, 256), F32)
        if a < 64:
            return above(56 * k + a - 8, n)
        return get(own, 64 * k + a - 64, n) if a < 128 else below(56 * k + a - 128, n)

    for a, n in chunks(0, 192, 8):
        put(wet_ref, PAD + a, jnp.where(window(0, a, n) > 0, 1.0, 0.0))
        put(b0, a, window(2, a, n))
    for a, n in chunks(0, 192, 8):
        wet = get(wet_ref, PAD + a, n)
        east = window(0, a, n) * from_east(wet, 1)
        south = window(1, a, n) * get(wet_ref, PAD + a + 1, n)
        put(co0, a, east, EAST)
        put(co0, a, from_west(east, 1), WEST)
        put(co0, a, south, SOUTH)
        put(south_ref, PAD + a, south)
        put(co0, a, wet * WET_MASS + (1.0 - wet), MASS)
    edges = ((63, above(175, 1), get(own, 192, 1)), (127, get(own, 255, 1), below(168, 1)))
    for row, here, next_row in edges:
        flow = get(co0, row, 1, SOUTH) * (here - next_row)
        put(b0, row, get(b0, row, 1) - flow)
        put(b0, row + 1, get(b0, row + 1, 1) + flow)
    for a, n in chunks(0, 192):
        put(co0, a, get(south_ref, PAD + a - 1, n), NORTH)
    set_rate(co0, 192)
    coarsen(co0, co1, 96, 1)
    set_rate(co1, 96)
    coarsen(co1, co2, 48, 2)
    set_rate(co2, 48)
    coarsen(co2, co3, 24, 4)
    set_rate(co3, 24)
    first_sweep(t0, co0, b0, 8, 184)
    sweep(t0, v0, co0, b0, 8, 184, 1)
    residual(v0, r0, co0, b0, 8, 184, 1)
    descend(
        v1, v2, b1, b2, b3, (co0, co1, co2), (r0, r1, r2), (t0, t1, t2), ((0, 192), (0, 96), (0, 48), (16, 32))
    )
    slot = lanes((8, 128)) & 7
    values = (
        b3[0, 8:16, :],
        co3[MASS, 0, 8:16, :],
        co3[EAST, 0, 8:16, :],
        co3[SOUTH, 0, 8:16, :],
        diagonal(co3, 8, 8)[:, :128],
    )
    out = jnp.zeros((8, 128), F32)
    for k, value in enumerate(values):
        out = jnp.where(slot == k, value, out)
    packed[...] = out


def fan(own, first, second, responded, out):
    even = lax.rem(lax.axis_index("x"), 2) == 0
    east = jnp.where(even, first[...], second[...])
    west = jnp.where(even, second[...], first[...])
    slot = lanes((8, 128)) & 7
    one = jnp.where(slot < 5, own[...], pltpu.roll(west, 5, 1))
    two = jnp.where(slot < 2, pltpu.roll(west, 125, 1), pltpu.roll(east, 2, 1))
    two = jnp.where(slot == 7, responded[...], two)
    for g in range(out.shape[0]):
        out[g, 0] = one
        out[g, 1] = two


def ascend(coarse, bases, sources, to, temp, co):
    ranges = ((32, 160), (8, 88), (0, 48))
    for level in (2, 1, 0):
        low, high = ranges[level]
        step = 1 << level
        prolong(coarse, bases[level], to[level], low, high)
        sweep(to[level], temp[level], co[level], sources[level], low, high, step)
        sweep(temp[level], to[level], co[level], sources[level], low, high, step)
        coarse = to[level]


def second_descent(start, source, kept, rest, temp, co):
    v0, v1, v2, b1, b2, b3 = kept
    sweep(start, temp[0], co[0], source, 32, 160, 1)
    sweep(temp[0], v0, co[0], source, 32, 160, 1)
    residual(v0, rest[0], co[0], source, 32, 160, 1)
    descend(v1, v2, b1, b2, b3, co, rest, temp, ((32, 160), (16, 80), (8, 40), (16, 32)))


def response(co0, co1, co2, co3, state, packed, *temps):
    v0, v1, v2, b1, b2, _ = state_of(state)
    t0, s0, t1, s1, t2, s2, v3, s3, r0, r1, r2, b3 = temps
    put(v3, PAD, jnp.ones((24, 256), F32))
    sweep(v3, s3, co3, None, 0, 24, 8)
    sweep(s3, v3, co3, None, 0, 24, 8)
    none, co = (None, None, None), (co0, co1, co2)
    ascend(v3, none, none, (t0, t1, t2), (s0, s1, s2), co)
    second_descent(t0, None, (v0, v1, v2, b1, b2, b3), (r0, r1, r2), (s0, s1, s2), co)
    packed[...] = b3[0, 8:16, :]


def neighbours():
    group, x = lax.axis_index("grp"), lax.axis_index("x")
    inner_west, inner_east = x > 0, x < 3
    return group, x, inner_west, inner_east, jnp.where(inner_west, x - 1, 3), jnp.where(inner_east, x + 1, 0)


def spread(x, slot):
    at = jnp.bitwise_or(jnp.bitwise_and(lanes(x.shape), 120), slot)
    return jnp.take_along_axis(x, at, axis=1, mode="promise_in_bounds")


def inner_part(wide, to):
    to[0, pl.ds(PAD, 24), :] = wide[1, pl.ds(PAD + 8, 24), :]
    low = lanes((24, 128)) < 64
    to[1, pl.ds(PAD, 24), :] = jnp.where(low, wide[2, pl.ds(PAD + 8, 24), :], wide[0, pl.ds(PAD + 8, 24), :])


def solve_coarse(b3, b4, co3, co4, v3, s3, v4, s4, rest, shift):
    first_sweep(s3, co3, b3, 0, 40)
    sweep(s3, v3, co3, b3, 0, 40, 8)
    residual(v3, rest, co3, b3, 0, 40, 8)
    restrict(rest, b4, 0, 48, 8)
    first_sweep(s4, co4, b4, 0, 24)
    sweep(s4, v4, co4, b4, 0, 24, 16)
    sweep(v4, s4, co4, b4, 0, 24, 16)
    sweep(s4, v4, co4, b4, 0, 24, 16)
    if shift is not None:
        put(v4, PAD, get(v4, PAD, 24) + shift)
    prolong(v4, v3, v3, 0, 40)
    sweep(v3, s3, co3, b3, 8, 32, 8)
    sweep(s3, v3, co3, b3, 8, 32, 8)


def second_leg(gathered, responded, co0, co1, co2, before, co3, co4, after, packed, *temps):
    v0, v1, v2, b1, b2, b0 = state_of(before)
    v0a, v1a, v2a, b1a, b2a, _ = state_of(after)
    (t0, s0, t1, s1, t2, s2, r0, r1, r2, e3, bn, b3, b4, v3, s3, w3, v4, s4, r3, south_ref) = temps
    group = lax.axis_index("grp")
    for t in range(5):
        at = group + (t - 2)
        valid = jnp.logical_and(at >= 0, at < 8).astype(F32)
        at = jnp.clip(at, 0, 7)
        one, two = gathered[at, 0] * valid, gathered[at, 1] * valid

        def wide(k):
            west = spread(one, 5 + k) if k < 3 else spread(two, k - 3)
            return jnp.concatenate([west, spread(one, k), spread(two, 2 + k)], axis=1)

        row = 8 * t
        put(b3, row, wide(0))
        put(co3, row, wide(1), MASS)
        east = wide(2)
        put(co3, row, east, EAST)
        put(co3, row, from_west(east, 8), WEST)
        south = wide(3)
        put(co3, row, south, SOUTH)
        put(south_ref, PAD + row, south)
        d = wide(4)
        put(co3, row, RELAX / jnp.where(d > 0, d, 1.0), RATE)
    for a, n in chunks(0, 40):
        put(co3, a, get(south_ref, PAD + a - 1, n), NORTH)
    coarsen(co3, co4, 20, 8)
    set_rate(co4, 24)

    put(v4, PAD, jnp.ones((24, 384), F32))
    for here, there in ((v4, s4), (s4, v4), (v4, s4), (s4, v4)):
        sweep(here, there, co4, None, 0, 24, 16)
    prolong(v4, None, w3, 0, 40)
    sweep(w3, s3, co3, None, 8, 32, 8)
    sweep(s3, w3, co3, None, 8, 32, 8)
    weight = w3[1, pl.ds(PAD + 16, 8), :]

    solve_coarse(b3, b4, co3, co4, v3, s3, v4, s4, r3, None)
    inner_part(v3, e3)
    co = (co0, co1, co2)
    ascend(e3, (v0, v1, v2), (b0, b1, b2), (t0, t1, t2), (s0, s1, s2), co)
    second_descent(t0, b0, (v0a, v1a, v2a, b1a, b2a, bn), (r0, r1, r2), (s0, s1, s2), co)
    result = bn[0, 8:16, :]
    slot = lanes((8, 128)) & 7
    out = jnp.where(slot == 0, result, jnp.where(slot == 1, responded[...], 0.0))
    mass = co3[MASS, 1, 16:24, :]
    sums = (mass, weight * b3[1, 16:24, :], weight * result, weight * responded[...])
    for k, value in enumerate(sums):
        out = jnp.where(slot == 2 + k, value, out)
    for z in range(packed.shape[0]):
        packed[z] = out


def relay(gathered, out):
    z = lax.axis_index("z")
    last = gathered.shape[0] - 1
    own = gathered[z]
    before = gathered[jnp.maximum(z - 1, 0)]
    after = gathered[jnp.minimum(z + 1, last)]
    total = gathered[0]
    for k in range(1, last + 1):
        total = total + gathered[k]
    slot = lanes((8, 128)) & 7
    value = jnp.where(slot < 2, own, jnp.where(slot < 4, pltpu.roll(before, 2, 1), pltpu.roll(after, 4, 1)))
    folded = total + pltpu.roll(total, 4, 0)
    top = lax.broadcasted_iota(jnp.int32, (8, 128), 0) < 4
    six = jnp.where(top, pltpu.roll(folded, 4, 1), pltpu.roll(folded, 3, 1))
    seven = jnp.where(top, pltpu.roll(folded, 3, 1), pltpu.roll(folded, 2, 1))
    value = jnp.where(slot < 6, value, jnp.where(slot == 6, six, seven))
    for k in range(out.shape[0]):
        out[k] = value


def third_leg(gathered, own, co0, co1, co2, before, co3, co4, after, beside, *others):
    b0 = state_of(before)[5]
    v0a, v1a, v2a, b1a, b2a, _ = state_of(after)
    v0b, v1b, v2b, b1b, b2b, _ = state_of(beside)
    (surface, rest, *temps) = others
    (t0, s0, c0, t1, s1, c1, d1, t2, s2, c2, d2, e3, b3, b4, v3, s3, v4, s4, r3) = temps
    total = gathered[0]
    for k in range(1, gathered.shape[0]):
        total = total + gathered[k]
    slot = lanes((8, 128)) & 7
    top = lax.broadcasted_iota(jnp.int32, (8, 128), 0) < 4

    def whole(k):
        kept = jnp.where((slot == 6 + k // 2) & (top if k % 2 == 0 else ~top), total, 0.0)
        return jnp.sum(jnp.sum(kept, axis=0, keepdims=True), axis=1, keepdims=True)

    mass, sum1, sum2a, sum2b = (whole(k) for k in range(4))
    shift1 = RELAX * sum1 / mass
    shift2 = RELAX * (sum2a + shift1 * sum2b) / mass

    group, x, inner_west, inner_east, at_west, at_east = neighbours()
    for t in range(5):
        g = 4 * jnp.clip(group + (t - 2), 0, 7)
        w, o, e = gathered[g + at_west], gathered[g + x], gathered[g + at_east]
        w = jnp.where(inner_west, w, pltpu.roll(w, 126, 1))
        e = jnp.where(inner_east, e, pltpu.roll(e, 124, 1))
        both = [spread(part + shift1 * from_east(part, 1), 0) for part in (w, o, e)]
        put(b3, 8 * t, jnp.concatenate(both, axis=1))
    solve_coarse(b3, b4, co3, co4, v3, s3, v4, s4, r3, shift2)
    inner_part(v3, e3)

    def combine(to, first, second, offset, low, high):
        for a, n in chunks(offset + low, offset + high):
            put(to, a, get(first, a, n) + shift1 * get(second, a, n))

    combine(c2, v2a, v2b, PAD, 8, 40)
    combine(d2, b2a, b2b, 0, 8, 40)
    combine(c1, v1a, v1b, PAD, 24, 72)
    combine(d1, b1a, b1b, 0, 24, 72)
    combine(c0, v0a, v0b, PAD, 56, 136)
    prolong(e3, c2, t2, 8, 40)
    sweep(t2, s2, co2, d2, 8, 40, 4)
    sweep(s2, t2, co2, d2, 8, 40, 4)
    prolong(t2, c1, t1, 24, 72)
    sweep(t1, s1, co1, d1, 24, 72, 2)
    sweep(s1, t1, co1, d1, 24, 72, 2)
    prolong(t1, c0, t0, 56, 136)
    sweep(t0, s0, co0, b0, 56, 136, 1)
    sweep(s0, t0, co0, b0, 56, 136, 1)
    surface[...] = own[0, pl.ds(192, 64), :] + t0[0, pl.ds(PAD + 64, 64), :]
    for a, n in chunks(64, 128):
        _, out = operate(t0, co0, a, n, 1)
        rest[a - 64 : a - 64 + n, :] = b0[0, a : a + n, :] - out[:, :128]


def swaps(start, count):
    low = range(start, count - 1, 2)
    return [(i, i + 1) for i in low] + [(i + 1, i) for i in low]


def shards(right_side, previous, east_face, south_face, wet_mask):
    dev = ("z", "x")
    own, first, second = call(
        prepare,
        (scratch(4, 64, 128), scratch(2, 64, 128), scratch(2, 64, 128)),
        [*[scratch(64, 128)] * 4, pltpu.VMEM((64, 128), jnp.int32), pltpu.SemaphoreType.DMA((5,))],
        right_side,
        previous,
        east_face,
        south_face,
        wet_mask,
        at=pltpu.HBM,
        room=60,
    )
    first = lax.ppermute(first, dev, swaps(0, 64))
    second = lax.ppermute(second, dev, swaps(1, 64))
    own, near, far = call(
        widen,
        (field(2, 256, 128), field(2, 176, 128), field(2, 176, 128)),
        [scratch(2, 80, 128)] * 3,
        own,
        second,
        first,
    )
    far = lax.ppermute(far, "grp", swaps(1, 8))
    near = lax.ppermute(near, "grp", swaps(0, 8))

    def rows(count, planes=2):
        return field(planes, count, 128)

    def shifted(count, planes=2):
        return field(planes, count + 2 * PAD, 128)

    def as_scratch(*fields):
        return [scratch(*f.shape) for f in fields]

    co = [field(6, 2, count, 128) for count in (192, 96, 48, 24)]
    fine = [shifted(count) for count in (192, 96, 48)]
    sources = [rows(count) for count in (192, 96, 48)]
    state = rows(STATE_ROWS)
    *kept, near, packed = call(
        first_leg,
        (*co[:3], state, co[3], field(8, 128)),
        as_scratch(fine[0], fine[0], *fine, *sources, rows(24)),
        own,
        far,
        near,
    )
    first = lax.ppermute(packed, dev, swaps(0, 64))
    second = lax.ppermute(packed, dev, swaps(1, 64))
    beside, responded = call(
        response,
        (state, field(8, 128)),
        as_scratch(*[f for f in fine for _ in range(2)], shifted(24), shifted(24), *sources, rows(24)),
        *kept[:3],
        near,
        cycles=3000,
    )
    gathered = call(fan, field(8, 2, 8, 128), [], packed, first, second, responded)
    gathered = lax.all_to_all(gathered, "grp", 0, 0, tiled=True)
    coarse = [shifted(40, 3), shifted(40, 3), shifted(40, 3), shifted(24, 3), shifted(24, 3)]
    *second, packed = call(
        second_leg,
        (field(6, 3, 40, 128), field(6, 3, 24, 128), state, field(16, 8, 128)),
        as_scratch(
            *[f for f in fine for _ in range(2)],
            *sources,
            shifted(24),
            rows(24),
            rows(40, 3),
            rows(24, 3),
            *coarse,
            rows(48, 3),
            shifted(40, 3),
        ),
        gathered,
        responded,
        *kept,
    )
    gathered = lax.all_to_all(packed, "z", 0, 0, tiled=True)
    gathered = call(relay, field(32, 8, 128), [], gathered)
    gathered = lax.all_to_all(gathered, ("grp", "x"), 0, 0, tiled=True)
    surface, rest = call(
        third_leg,
        (field(64, 128), field(64, 128)),
        as_scratch(
            *[shifted(192)] * 3,
            *[shifted(96)] * 3,
            rows(96),
            *[shifted(48)] * 3,
            rows(48),
            shifted(24),
            rows(40, 3),
            rows(24, 3),
            shifted(40, 3),
            shifted(40, 3),
            shifted(24, 3),
            shifted(24, 3),
            rows(48, 3),
        ),
        gathered,
        own,
        *kept,
        *second,
        beside,
    )
    return surface, rest


def solution(mesh):
    split = Mesh(mesh.devices.reshape(8, 16, 4), ("grp", "z", "x"))
    placed = P("grp", ("z", "x"))
    return jax.shard_map(shards, mesh=split, in_specs=(placed,) * 5, out_specs=(placed,) * 2, check_vma=False)
```
